32 devices in a mesh: dap: 16 (over z, y, core), dp: 2 (over x).
Axes of the slice: x: 2, y: 2, z: 4, core: 2. Of those that a mesh axis runs over, the one named last changes fastest.
Arguments:
- alignment_embedding: bfloat16 [32, 16, 256], P('dp', 'dap'), parts along dimension 0, may hold values from -6 to 6
- alignment_existing_flags: int32 [32, 16], P('dp', 'dap'), parts along dimension 0, may hold values 0 or 1
- couple_embedding: bfloat16 [32, 16, 128], P(('dp', 'dap')), parts along dimension 0, may hold values from -6 to 6
- alignment_scaling_factor: float32 [256], replicated, may hold values from 0.1 to 1.9
- couple_scaling_factor: float32 [128], replicated, may hold values from 0.1 to 1.9
- request_matrix: bfloat16 [256, 256], replicated, may hold values from -0.375 to 0.375
- lookup_matrix: bfloat16 [256, 256], replicated, may hold values from -0.375 to 0.375
- content_matrix: bfloat16 [256, 256], replicated, may hold values from -0.375 to 0.375
- switch_matrix: bfloat16 [256, 256], replicated, may hold values from -0.375 to 0.375
- final_projection_matrix: bfloat16 [256, 256], replicated, may hold values from -0.375 to 0.375
- couple_to_headterm_matrix: bfloat16 [128, 8], replicated, may hold values from -30 to 30
- increment_adjoint: bfloat16 [32, 16, 256], P('dp', 'dap'), parts along dimension 0, may hold values from -48 to 48
Outputs:
- alignment_increment: bfloat16 [32, 16, 256], P('dp', 'dap'), parts along dimension 0
- alignment_adjoint: bfloat16 [32, 16, 256], P('dp', 'dap'), parts along dimension 0
- couple_adjoint: bfloat16 [32, 16, 128], P(('dp', 'dap')), parts along dimension 0
- d_w_query: float32 [512, 256], P('dp'), parts along dimension 0
- d_w_key: float32 [512, 256], P('dp'), parts along dimension 0
- d_w_value: float32 [512, 256], P('dp'), parts along dimension 0
- d_w_gate: float32 [512, 256], P('dp'), parts along dimension 0
- d_w_out: float32 [512, 256], P('dp'), parts along dimension 0
- couple_headterm_adjoint: float32 [256, 8], P('dp'), parts along dimension 0
- d_msa_gain: float32 [512], P('dp'), parts along dimension 0
- couple_scaling_adjoint: float32 [256], P('dp'), parts along dimension 0
The draws below stay inside these ranges and needn't reach their ends.
There are 2 independent parts, one for each index of `dp`. The reference program is written for one: setup_inputs(seed, part) draws one part's arguments, and reference() takes and returns one part's arrays. A program takes and returns all parts, laid end to end along the dimension named above; an argument that names none is the same for every part. Nothing has to cross between parts.
All inputs are finite; a program needn't handle non-finite values. No bound on the sum of `alignment_existing_flags` on one device may be relied on, other than what follows from the above.
Results may differ from the reference program's by a relative error of at most 0.012.
The reference program's roundings to bfloat16 on the way count: a program that leaves them out, or rounds other values in their place, can miss the bound.
Values may be sent and summed in bfloat16 or wider, within the bound.
A program may use at most 64 MiB of HBM per device.

```python
import jax
import jax.numpy as jnp
from jax import lax

ALIGN_FEATURES = 256
CZ = 128
HEAD_NUMBER = 8
HEAD_DIMENSION = 32
WINDOW_AMINO = 16
ALIGN_DEPTH = 16


def draw_couple_to_headterm_matrix(key, part):
    leading_element, trailing_element = jax.random.split(jax.random.fold_in(key, 11))
    lower_bound_index = jax.random.normal(leading_element, (CZ, HEAD_NUMBER), jnp.float32) * CZ ** (-0.5)
    factors_list = jnp.exp(jax.random.uniform(trailing_element, (1, HEAD_NUMBER), jnp.float32, -0.3, 0.7))
    return jnp.clip(lower_bound_index * factors_list, -30.0, 30.0).astype(jnp.bfloat16)


def draw_increment_adjoint(key, part):
    leading_element = jax.random.fold_in(jax.random.fold_in(key, 23), 0)
    lower_bound_index = jax.random.normal(leading_element, (ALIGN_DEPTH, WINDOW_AMINO, ALIGN_FEATURES), jnp.float32)
    location_index = jnp.arange(ALIGN_DEPTH, dtype=jnp.float32) / max(ALIGN_DEPTH - 1, 1)
    factors_list = (3.0 ** location_index)[:, None, None] * jnp.ones((ALIGN_DEPTH, WINDOW_AMINO, 1), jnp.float32)
    return jnp.clip(lower_bound_index * factors_list, -48.0, 48.0).astype(jnp.bfloat16)


def place_ends(array, own_key, least, top_value):
    dims = array.shape
    spot = [jax.random.randint(jax.random.fold_in(own_key, axis), (), 0, dims[axis]) for axis in range(len(dims))]
    array = array.at[tuple(spot)].set(least)
    longest = dims.index(max(dims))
    spot[longest] = (spot[longest] + 1) % dims[longest]
    return array.at[tuple(spot)].set(top_value)


def levels(stream_key, dims, cuts, least, largest):
    def one(axis_at, parts):
        steps = jax.random.uniform(jax.random.fold_in(jax.random.fold_in(stream_key, 6), axis_at), (parts,), jnp.float32, least / len(cuts), largest / len(cuts))
        return jnp.repeat(jnp.exp(steps), dims[axis_at] // parts).reshape((-1,) + (1,) * (len(dims) - axis_at - 1))

    level = one(*cuts[0])
    for cut in cuts[1:]:
        level = level * one(*cut)
    return level


def normal_values(key, dims, width, most, cuts=(), held_as=jnp.bfloat16):
    array = width * jax.random.normal(key, dims, jnp.float32)
    if cuts:
        array = array * levels(key, dims, cuts, -0.22, 0.18)
    return jnp.clip(array, -most, most).astype(held_as)


def setup_inputs(seed: int = 0, part: int = 0) -> dict:
    seeds = jax.random.split(jax.random.key(seed), 13)
    part_keys = jax.random.split(jax.random.fold_in(seeds[12], part), 13)
    return {
        "alignment_embedding": normal_values(part_keys[0], (ALIGN_DEPTH, WINDOW_AMINO, ALIGN_FEATURES), 1.0, 6.0, ((1, 16),)),
        "alignment_existing_flags": place_ends((jax.random.randint(part_keys[1], (ALIGN_DEPTH, WINDOW_AMINO), 0, 4) < 3).astype(jnp.int32), jax.random.fold_in(part_keys[1], 1), 0, 1),
        "couple_embedding": normal_values(part_keys[2], (WINDOW_AMINO, WINDOW_AMINO, CZ), 1.0, 6.0, ((0, 16),)),
        "alignment_scaling_factor": jnp.clip(1.0 + 0.18 * jax.random.normal(seeds[3], (ALIGN_FEATURES,), jnp.float32), 0.1, 1.9),
        "couple_scaling_factor": jnp.clip(1.0 + 0.18 * jax.random.normal(seeds[4], (CZ,), jnp.float32), 0.1, 1.9),
        "request_matrix": normal_values(seeds[5], (ALIGN_FEATURES, HEAD_NUMBER * HEAD_DIMENSION), ALIGN_FEATURES ** -0.5, 0.375),
        "lookup_matrix": normal_values(seeds[6], (ALIGN_FEATURES, HEAD_NUMBER * HEAD_DIMENSION), ALIGN_FEATURES ** -0.5, 0.375),
        "content_matrix": normal_values(seeds[7], (ALIGN_FEATURES, HEAD_NUMBER * HEAD_DIMENSION), ALIGN_FEATURES ** -0.5, 0.375),
        "switch_matrix": normal_values(seeds[8], (ALIGN_FEATURES, HEAD_NUMBER * HEAD_DIMENSION), ALIGN_FEATURES ** -0.5, 0.375),
        "final_projection_matrix": normal_values(seeds[9], (HEAD_NUMBER * HEAD_DIMENSION, ALIGN_FEATURES), (HEAD_NUMBER * HEAD_DIMENSION) ** -0.5, 0.375),
        "couple_to_headterm_matrix": draw_couple_to_headterm_matrix(jax.random.fold_in(seeds[12], 71), part),
        "increment_adjoint": draw_increment_adjoint(jax.random.fold_in(jax.random.fold_in(seeds[12], part), 71), part),
    }


EPS = 1e-05

def standardise_features(value, gain):
    mean = lax.optimization_barrier(jnp.mean(value, axis=-1, keepdims=True))
    centered = value - mean
    variance = lax.optimization_barrier(jnp.mean(centered * centered, axis=-1, keepdims=True))
    reciprocal_spread = lax.rsqrt(variance + EPS)
    standardised_lines = centered * reciprocal_spread
    return (standardised_lines, reciprocal_spread, standardised_lines * gain)

def standardise_features_adjoint(upstream_gradient, standardised_lines, reciprocal_spread, gain):
    rescaled_request = upstream_gradient * gain
    return reciprocal_spread * (rescaled_request - lax.optimization_barrier(jnp.mean(rescaled_request, axis=-1, keepdims=True)) - standardised_lines * lax.optimization_barrier(jnp.mean(rescaled_request * standardised_lines, axis=-1, keepdims=True)))

def tensor_product(left, right):
    return jnp.dot(left.T, right, preferred_element_type=jnp.float32)

def onward_one_line(alignment_line_content, line_filter_flags, couple_headwise_terms, alignment_scaling_factor, request_matrix, lookup_matrix, content_matrix, switch_matrix, final_projection_matrix):
    element_number = alignment_line_content.shape[0]
    standardised_lines, reciprocal_spread, rescaled_request = standardise_features(alignment_line_content.astype(jnp.float32), alignment_scaling_factor)
    input_arrays = rescaled_request.astype(jnp.bfloat16)
    query = (jnp.dot(input_arrays, request_matrix, preferred_element_type=jnp.float32) * HEAD_DIMENSION ** (-0.5)).astype(jnp.bfloat16)
    keys = jnp.dot(input_arrays, lookup_matrix, preferred_element_type=jnp.float32).astype(jnp.bfloat16)
    values = jnp.dot(input_arrays, content_matrix, preferred_element_type=jnp.float32).astype(jnp.bfloat16)
    gate_sigmoid = jax.nn.sigmoid(jnp.dot(input_arrays, switch_matrix, preferred_element_type=jnp.float32))
    query = query.reshape(element_number, HEAD_NUMBER, HEAD_DIMENSION)
    keys = keys.reshape(element_number, HEAD_NUMBER, HEAD_DIMENSION)
    values = values.reshape(element_number, HEAD_NUMBER, HEAD_DIMENSION)
    scores = jnp.einsum('ihd,jhd->ihj', query.astype(jnp.float32), keys.astype(jnp.float32))
    scores = scores + couple_headwise_terms.astype(jnp.float32) + (1000000000.0 * (line_filter_flags.astype(jnp.float32) - 1.0))[None, None, :]
    probs = jax.nn.softmax(scores, axis=-1)
    probs_low = probs.astype(jnp.bfloat16)
    attention_probs = jnp.einsum('ihj,jhd->ihd', probs_low.astype(jnp.float32), values.astype(jnp.float32)).reshape(element_number, HEAD_NUMBER * HEAD_DIMENSION)
    weighted_values = (gate_sigmoid * attention_probs).astype(jnp.bfloat16)
    alignment_increment = jnp.dot(weighted_values, final_projection_matrix, preferred_element_type=jnp.float32).astype(jnp.bfloat16)
    kept_intermediates = (standardised_lines, reciprocal_spread, input_arrays, query, keys, values, gate_sigmoid, attention_probs, weighted_values, probs)
    return (alignment_increment, kept_intermediates)

def reverse_one_line(line_adjoint_routine, kept_intermediates, alignment_scaling_factor, request_matrix, lookup_matrix, content_matrix, switch_matrix, final_projection_matrix):
    standardised_lines, reciprocal_spread, input_arrays, query, keys, values, gate_sigmoid, attention_probs, weighted_values, probs = kept_intermediates
    element_number = line_adjoint_routine.shape[0]
    probs_low = probs.astype(jnp.bfloat16)
    upstream_gradient = jnp.dot(line_adjoint_routine, final_projection_matrix.T, preferred_element_type=jnp.float32)
    d_attn = (upstream_gradient * gate_sigmoid).astype(jnp.bfloat16)
    gate_logit_gradient = (upstream_gradient * attention_probs * gate_sigmoid * (1.0 - gate_sigmoid)).astype(jnp.bfloat16)
    d_attn_heads = d_attn.reshape(element_number, HEAD_NUMBER, HEAD_DIMENSION)
    d_probs = jnp.einsum('ihd,jhd->ihj', d_attn_heads.astype(jnp.float32), values.astype(jnp.float32))
    affinity_adjoint = probs * (d_probs - lax.optimization_barrier(jnp.sum(probs * d_probs, axis=-1, keepdims=True)))
    d_low = affinity_adjoint.astype(jnp.bfloat16).astype(jnp.float32)
    query_gradient = (jnp.einsum('ihj,jhd->ihd', d_low, keys.astype(jnp.float32)) * HEAD_DIMENSION ** (-0.5)).astype(jnp.bfloat16).reshape(element_number, HEAD_NUMBER * HEAD_DIMENSION)
    key_gradient = jnp.einsum('ihj,ihd->jhd', d_low, query.astype(jnp.float32)).astype(jnp.bfloat16).reshape(element_number, HEAD_NUMBER * HEAD_DIMENSION)
    value_gradient = jnp.einsum('ihj,ihd->jhd', probs_low.astype(jnp.float32), d_attn_heads.astype(jnp.float32)).astype(jnp.bfloat16).reshape(element_number, HEAD_NUMBER * HEAD_DIMENSION)
    argument_adjoints = jnp.dot(query_gradient, request_matrix.T, preferred_element_type=jnp.float32)
    argument_adjoints = argument_adjoints + jnp.dot(key_gradient, lookup_matrix.T, preferred_element_type=jnp.float32)
    argument_adjoints = argument_adjoints + jnp.dot(value_gradient, content_matrix.T, preferred_element_type=jnp.float32)
    argument_adjoints = argument_adjoints + jnp.dot(gate_logit_gradient, switch_matrix.T, preferred_element_type=jnp.float32)
    line_adjoint = standardise_features_adjoint(argument_adjoints, standardised_lines, reciprocal_spread, alignment_scaling_factor).astype(jnp.bfloat16)
    matrix_adjoints = (tensor_product(input_arrays, query_gradient), tensor_product(input_arrays, key_gradient), tensor_product(input_arrays, value_gradient), tensor_product(input_arrays, gate_logit_gradient), tensor_product(weighted_values, line_adjoint_routine), lax.optimization_barrier(jnp.sum(argument_adjoints * standardised_lines, axis=0)))
    return (line_adjoint, affinity_adjoint, matrix_adjoints)

def reference(alignment_embedding, alignment_existing_flags, couple_embedding, alignment_scaling_factor, couple_scaling_factor, request_matrix, lookup_matrix, content_matrix, switch_matrix, final_projection_matrix, couple_to_headterm_matrix, increment_adjoint):
    pair_hat, pair_inv, pair_scaled = standardise_features(couple_embedding.astype(jnp.float32), couple_scaling_factor)
    pair_ln = pair_scaled.astype(jnp.bfloat16)
    couple_headwise_terms = jnp.einsum('ijc,ch->ihj', pair_ln.astype(jnp.float32), couple_to_headterm_matrix.astype(jnp.float32), precision=lax.Precision.HIGHEST).astype(jnp.bfloat16)

    def loop_step(carry, loop_elements):
        bias_sum, subtotal_list = carry
        alignment_increment, kept_intermediates = onward_one_line(loop_elements[0], loop_elements[1], couple_headwise_terms, alignment_scaling_factor, request_matrix, lookup_matrix, content_matrix, switch_matrix, final_projection_matrix)
        line_adjoint, affinity_adjoint, matrix_adjoints = reverse_one_line(loop_elements[2], kept_intermediates, alignment_scaling_factor, request_matrix, lookup_matrix, content_matrix, switch_matrix, final_projection_matrix)
        subtotal_list = tuple((a + b for a, b in zip(subtotal_list, matrix_adjoints)))
        return ((bias_sum + affinity_adjoint, subtotal_list), (alignment_increment, line_adjoint))
    span_length = HEAD_NUMBER * HEAD_DIMENSION
    blank_matrix = (jnp.zeros((ALIGN_FEATURES, span_length), jnp.float32), jnp.zeros((ALIGN_FEATURES, span_length), jnp.float32), jnp.zeros((ALIGN_FEATURES, span_length), jnp.float32), jnp.zeros((ALIGN_FEATURES, span_length), jnp.float32), jnp.zeros((span_length, ALIGN_FEATURES), jnp.float32), jnp.zeros((ALIGN_FEATURES,), jnp.float32))
    beginning_shift = (jnp.zeros((WINDOW_AMINO, HEAD_NUMBER, WINDOW_AMINO), jnp.float32), blank_matrix)
    (additive_term_adjoint, subtotal_list), (alignment_increment, alignment_adjoint) = lax.scan(loop_step, beginning_shift, (alignment_embedding, alignment_existing_flags, increment_adjoint))
    d_pln = jnp.einsum('ihj,ch->ijc', additive_term_adjoint, couple_to_headterm_matrix.astype(jnp.float32), precision=lax.Precision.HIGHEST)
    couple_headterm_adjoint = jnp.einsum('ijc,ihj->ch', pair_ln.astype(jnp.float32), additive_term_adjoint, precision=lax.Precision.HIGHEST)
    couple_scaling_adjoint = lax.optimization_barrier(jnp.sum(d_pln * pair_hat, axis=(0, 1)))
    couple_adjoint = standardise_features_adjoint(d_pln, pair_hat, pair_inv, couple_scaling_factor).astype(jnp.bfloat16)
    return (alignment_increment, alignment_adjoint, couple_adjoint, subtotal_list[0], subtotal_list[1], subtotal_list[2], subtotal_list[3], subtotal_list[4], couple_headterm_adjoint, subtotal_list[5], couple_scaling_adjoint)
```

```python
import jax
import jax.numpy as jnp
from jax import lax
from jax.experimental import pallas as pl
from jax.experimental.pallas import tpu as pltpu
from jax.sharding import PartitionSpec as P

ALIGN_FEATURES = 256
HEAD_NUMBER = 8
HEAD_DIMENSION = 32


EPS = 1e-05


def standardise_features(value, gain):
    mean = jnp.mean(value, axis=-1, keepdims=True)
    centered = value - mean
    variance = jnp.mean(centered * centered, axis=-1, keepdims=True)
    reciprocal_spread = lax.rsqrt(variance + EPS)
    standardised_lines = centered * reciprocal_spread
    return (standardised_lines, reciprocal_spread, standardised_lines * gain)


def standardise_features_adjoint(upstream_gradient, standardised_lines, reciprocal_spread, gain):
    rescaled_request = upstream_gradient * gain
    return reciprocal_spread * (
        rescaled_request
        - jnp.mean(rescaled_request, axis=-1, keepdims=True)
        - standardised_lines
        * jnp.mean(rescaled_request * standardised_lines, axis=-1, keepdims=True)
    )


def tensor_product(left, right):
    return lax.dot_general(
        left, right, (((0,), (0,)), ((), ())), preferred_element_type=jnp.float32
    )


def onward_one_line(
    alignment_line_content,
    line_filter_flags,
    couple_headwise_terms,
    alignment_scaling_factor,
    request_matrix,
    lookup_matrix,
    content_matrix,
    switch_matrix,
    final_projection_matrix,
):
    element_number = alignment_line_content.shape[0]
    standardised_lines, reciprocal_spread, rescaled_request = standardise_features(
        alignment_line_content.astype(jnp.float32), alignment_scaling_factor
    )
    input_arrays = rescaled_request.astype(jnp.bfloat16)
    query = (
        jnp.dot(input_arrays, request_matrix, preferred_element_type=jnp.float32)
        * HEAD_DIMENSION ** (-0.5)
    ).astype(jnp.bfloat16)
    keys = jnp.dot(input_arrays, lookup_matrix, preferred_element_type=jnp.float32).astype(
        jnp.bfloat16
    )
    values = jnp.dot(input_arrays, content_matrix, preferred_element_type=jnp.float32).astype(
        jnp.bfloat16
    )
    gate_sigmoid = jax.nn.sigmoid(
        jnp.dot(input_arrays, switch_matrix, preferred_element_type=jnp.float32)
    )
    query = query.reshape(element_number, HEAD_NUMBER, HEAD_DIMENSION)
    keys = keys.reshape(element_number, HEAD_NUMBER, HEAD_DIMENSION)
    values = values.reshape(element_number, HEAD_NUMBER, HEAD_DIMENSION)
    scores = jnp.einsum("ihd,jhd->ihj", query, keys, preferred_element_type=jnp.float32)
    scores = (
        scores
        + couple_headwise_terms.astype(jnp.float32)
        + (1000000000.0 * (line_filter_flags.astype(jnp.float32) - 1.0))[None, None, :]
    )
    probs = jax.nn.softmax(scores, axis=-1)
    probs_low = probs.astype(jnp.bfloat16)
    attention_probs = jnp.einsum(
        "ihj,jhd->ihd", probs_low, values, preferred_element_type=jnp.float32
    ).reshape(element_number, HEAD_NUMBER * HEAD_DIMENSION)
    weighted_values = (gate_sigmoid * attention_probs).astype(jnp.bfloat16)
    alignment_increment = jnp.dot(
        weighted_values, final_projection_matrix, preferred_element_type=jnp.float32
    ).astype(jnp.bfloat16)
    kept_intermediates = (
        standardised_lines,
        reciprocal_spread,
        input_arrays,
        query,
        keys,
        values,
        gate_sigmoid,
        attention_probs,
        weighted_values,
        probs,
    )
    return (alignment_increment, kept_intermediates)


def reverse_one_line(
    line_adjoint_routine,
    kept_intermediates,
    alignment_scaling_factor,
    request_matrix,
    lookup_matrix,
    content_matrix,
    switch_matrix,
    final_projection_matrix,
):
    (
        standardised_lines,
        reciprocal_spread,
        input_arrays,
        query,
        keys,
        values,
        gate_sigmoid,
        attention_probs,
        weighted_values,
        probs,
    ) = kept_intermediates
    element_number = line_adjoint_routine.shape[0]
    probs_low = probs.astype(jnp.bfloat16)
    upstream_gradient = lax.dot_general(
        line_adjoint_routine,
        final_projection_matrix,
        (((1,), (1,)), ((), ())),
        preferred_element_type=jnp.float32,
    )
    d_attn = (upstream_gradient * gate_sigmoid).astype(jnp.bfloat16)
    gate_logit_gradient = (
        upstream_gradient * attention_probs * gate_sigmoid * (1.0 - gate_sigmoid)
    ).astype(jnp.bfloat16)
    d_attn_heads = d_attn.reshape(element_number, HEAD_NUMBER, HEAD_DIMENSION)
    d_probs = jnp.einsum("ihd,jhd->ihj", d_attn_heads, values, preferred_element_type=jnp.float32)
    affinity_adjoint = probs * (d_probs - jnp.sum(probs * d_probs, axis=-1, keepdims=True))
    d_low = affinity_adjoint.astype(jnp.bfloat16)
    query_gradient = (
        (
            jnp.einsum("ihj,jhd->ihd", d_low, keys, preferred_element_type=jnp.float32)
            * HEAD_DIMENSION ** (-0.5)
        )
        .astype(jnp.bfloat16)
        .reshape(element_number, HEAD_NUMBER * HEAD_DIMENSION)
    )
    key_gradient = (
        jnp.einsum("ihj,ihd->jhd", d_low, query, preferred_element_type=jnp.float32)
        .astype(jnp.bfloat16)
        .reshape(element_number, HEAD_NUMBER * HEAD_DIMENSION)
    )
    value_gradient = (
        jnp.einsum("ihj,ihd->jhd", probs_low, d_attn_heads, preferred_element_type=jnp.float32)
        .astype(jnp.bfloat16)
        .reshape(element_number, HEAD_NUMBER * HEAD_DIMENSION)
    )
    backward_result = (((1,), (1,)), ((), ()))
    argument_adjoints = lax.dot_general(
        query_gradient, request_matrix, backward_result, preferred_element_type=jnp.float32
    )
    argument_adjoints = argument_adjoints + lax.dot_general(
        key_gradient, lookup_matrix, backward_result, preferred_element_type=jnp.float32
    )
    argument_adjoints = argument_adjoints + lax.dot_general(
        value_gradient, content_matrix, backward_result, preferred_element_type=jnp.float32
    )
    argument_adjoints = argument_adjoints + lax.dot_general(
        gate_logit_gradient, switch_matrix, backward_result, preferred_element_type=jnp.float32
    )
    line_adjoint = standardise_features_adjoint(
        argument_adjoints, standardised_lines, reciprocal_spread, alignment_scaling_factor
    ).astype(jnp.bfloat16)
    matrix_adjoints = (
        tensor_product(input_arrays, query_gradient),
        tensor_product(input_arrays, key_gradient),
        tensor_product(input_arrays, value_gradient),
        tensor_product(input_arrays, gate_logit_gradient),
        tensor_product(weighted_values, line_adjoint_routine),
        jnp.sum(argument_adjoints * standardised_lines, axis=0),
    )
    return (line_adjoint, affinity_adjoint, matrix_adjoints)


LANES = 128
ROW_TILE = 16


def whole_part_fits(alignment_embedding, couple_embedding):
    sequences, owned, _ = alignment_embedding.shape
    owned_pairs, residues, pair_channels = couple_embedding.shape
    devices = lax.axis_size("dap")
    return (
        owned == 1
        and owned_pairs == 1
        and devices == residues
        and devices % 4 == 0
        and HEAD_NUMBER * residues == LANES
        and pair_channels == LANES
        and sequences == residues
        and sequences % ROW_TILE == 0
    )


def gather_kernel(devices, msa_ref, flag_ref, pair_ref, grad_ref, all_ref, send_sem, recv_sem):
    me = lax.axis_index("dap")
    rows = msa_ref.shape[0]
    lanes = pair_ref.shape[1]
    planes = devices // 4
    core = lax.rem(me, 2)
    row = lax.rem(me // 2, 2)
    sibling = me + 1 - 2 * core
    across = me + 2 - 4 * row
    far = [lax.rem(me + 4 * k, devices) for k in range(1, planes)]
    far_across = [lax.rem(across + 4 * k, devices) for k in range(1, planes)]

    barrier = pltpu.get_barrier_semaphore()
    for peer in far + [across, sibling]:
        pl.semaphore_signal(
            barrier, inc=1, device_id={"dap": peer}, device_id_type=pl.DeviceIdType.MESH
        )
    all_ref[me, 0:rows, :] = msa_ref[...]
    all_ref[me, rows : 2 * rows, :] = grad_ref[...]
    all_ref[me, 2 * rows :, 0:lanes] = pair_ref[...]
    all_ref[me, 2 * rows :, lanes:] = jnp.broadcast_to(
        flag_ref[...].astype(jnp.float32), (rows, lanes)
    ).astype(jnp.bfloat16)
    pl.semaphore_wait(barrier, planes + 1)

    sent = []

    def send(slot, peer):
        copy = pltpu.make_async_remote_copy(
            src_ref=all_ref.at[slot],
            dst_ref=all_ref.at[slot],
            send_sem=send_sem.at[len(sent)],
            recv_sem=recv_sem.at[slot],
            device_id={"dap": peer},
            device_id_type=pl.DeviceIdType.MESH,
        )
        copy.start()
        sent.append(copy)

    def arrive(slot):
        pltpu.make_async_remote_copy(
            src_ref=all_ref.at[slot],
            dst_ref=all_ref.at[slot],
            send_sem=send_sem.at[0],
            recv_sem=recv_sem.at[slot],
            device_id={"dap": sibling},
            device_id_type=pl.DeviceIdType.MESH,
        ).wait_recv()

    for peer in far:
        send(me, peer)
    send(me, across)
    send(me, sibling)
    arrive(across)
    send(across, sibling)
    for slot in far:
        arrive(slot)
        send(slot, across)
        send(slot, sibling)
    for slot in far_across:
        arrive(slot)
        send(slot, sibling)
    sibling_across = sibling + 2 - 4 * row
    for k in range(planes):
        arrive(lax.rem(sibling + 4 * k, devices))
        arrive(lax.rem(sibling_across + 4 * k, devices))
    for copy in sent:
        copy.wait_send()


def iota(shape, dimension):
    return lax.broadcasted_iota(jnp.int32, shape, dimension)


def one_where(condition):
    return jnp.where(condition, 1.0, 0.0).astype(jnp.bfloat16)


def product(left, right, contract=((1,), (0,))):
    return lax.dot_general(left, right, (contract, ((), ())), preferred_element_type=jnp.float32)


OUTER = ((1,), (1,))
INNER = ((0,), (0,))


def split_product(left, right, contract=((1,), (0,)), split_left=True):
    wide = left if split_left else right
    upper = wide.astype(jnp.bfloat16)
    lower = (wide - upper.astype(jnp.float32)).astype(jnp.bfloat16)
    if split_left:
        return product(upper, right, contract) + product(lower, right, contract)
    return product(left, upper, contract) + product(left, lower, contract)


def over_group(value, width, combine):
    lane = iota(value.shape, 1)
    size = value.shape[1]
    step = 1
    while step < width:
        other = jnp.where(
            (lane // step) % 2 == 0,
            pltpu.roll(value, size - step, 1),
            pltpu.roll(value, step, 1),
        )
        value = combine(value, other)
        step *= 2
    return value


def part_kernel(
    all_ref,
    gain_ref,
    pair_gain_ref,
    request_ref,
    lookup_ref,
    content_ref,
    switch_ref,
    final_ref,
    headterm_ref,
    update_ref,
    adjoint_ref,
    pair_adjoint_ref,
    d_query_ref,
    d_key_ref,
    d_value_ref,
    d_gate_ref,
    d_out_ref,
    d_headterm_ref,
    d_gain_ref,
    d_pair_gain_ref,
    pair_rows_ref,
):
    me = lax.axis_index("dap")
    residues = all_ref.shape[0]
    sequences = all_ref.shape[1] // 3
    channels = all_ref.shape[2]
    tokens = residues * sequences
    span = HEAD_NUMBER * HEAD_DIMENSION
    columns = HEAD_NUMBER * residues
    gain = gain_ref[...]
    pair_gain = pair_gain_ref[...]

    pair_lanes = pair_gain.shape[1]
    pair_raw = all_ref[:, 2 * sequences :, 0:pair_lanes].reshape(residues * residues, pair_lanes)
    pair_hat, pair_inv, pair_scaled = standardise_features(
        pair_raw.astype(jnp.float32), pair_gain
    )
    pair_ln = pair_scaled.astype(jnp.bfloat16)
    spread = one_where(
        iota((HEAD_NUMBER, columns), 0) == iota((HEAD_NUMBER, columns), 1) // residues
    )
    headterm_wide = product(headterm_ref[...], spread).astype(jnp.bfloat16)
    pair_shape = (residues * residues, columns)
    same_key = iota(pair_shape, 0) % residues == iota(pair_shape, 1) % residues
    bias = jnp.sum(
        jnp.where(same_key, product(pair_ln, headterm_wide), 0.0).reshape(
            residues, residues, columns
        ),
        axis=1,
    )
    bias = bias.astype(jnp.bfloat16).astype(jnp.float32)

    flag_lane = iota((sequences, columns), 1) % residues
    flags = jnp.zeros((sequences, columns), jnp.float32)
    for j in range(residues):
        flags = jnp.where(
            flag_lane == j, all_ref[j, 2 * sequences :, pair_lanes:].astype(jnp.float32), flags
        )
    fill = 1000000000.0 * (flags - 1.0)

    square = (tokens, tokens)
    reorder = one_where(
        (iota(square, 0) // residues == iota(square, 1) % sequences)
        & (iota(square, 0) % residues == iota(square, 1) // sequences)
    )
    raw = product(reorder, all_ref[:, 0:sequences, :].reshape(tokens, channels))
    grad = product(
        reorder, all_ref[:, sequences : 2 * sequences, :].reshape(tokens, channels)
    ).astype(jnp.bfloat16)

    hat, inv, scaled = standardise_features(raw, gain)
    x = scaled.astype(jnp.bfloat16)
    query = (product(x, request_ref[...]) * HEAD_DIMENSION ** (-0.5)).astype(jnp.bfloat16)
    keys = product(x, lookup_ref[...]).astype(jnp.bfloat16)
    values = product(x, content_ref[...]).astype(jnp.bfloat16)
    gate = jax.nn.sigmoid(product(x, switch_ref[...]))
    upstream = product(grad, final_ref[...], OUTER)
    d_attn = (upstream * gate).astype(jnp.bfloat16)

    head_shape = (columns, span)
    own_head = iota(head_shape, 0) // residues == iota(head_shape, 1) // HEAD_DIMENSION
    own_head_one = one_where(own_head)

    def rows_of(value, s):
        return value[s * residues : (s + 1) * residues]

    def by_head(value):
        return jnp.concatenate([value] * HEAD_NUMBER, axis=0) * own_head_one

    def fold_heads(value):
        return jnp.sum(
            jnp.where(own_head, value, 0.0).reshape(HEAD_NUMBER, residues, span), axis=0
        )

    every = range(sequences)
    wide_keys = [by_head(rows_of(keys, s)) for s in every]
    wide_values = [by_head(rows_of(values, s)) for s in every]
    scores = jnp.concatenate(
        [
            product(rows_of(query, s), wide_keys[s], OUTER) + bias + fill[s : s + 1]
            for s in every
        ],
        axis=0,
    )
    scores = jnp.exp(scores - over_group(scores, residues, jnp.maximum))
    probs = scores / over_group(scores, residues, jnp.add)
    probs_low = probs.astype(jnp.bfloat16)
    d_probs = jnp.concatenate(
        [product(rows_of(d_attn, s), wide_values[s], OUTER) for s in every], axis=0
    )
    d_scores = probs * (d_probs - over_group(probs * d_probs, residues, jnp.add))
    d_low = d_scores.astype(jnp.bfloat16)
    attended = jnp.concatenate(
        [product(rows_of(probs_low, s), wide_values[s]) for s in every], axis=0
    )
    weighted = (gate * attended).astype(jnp.bfloat16)
    d_glog = (upstream * attended * gate * (1.0 - gate)).astype(jnp.bfloat16)
    d_query = jnp.concatenate(
        [product(rows_of(d_low, s), wide_keys[s]) for s in every], axis=0
    )
    d_query = (d_query * HEAD_DIMENSION ** (-0.5)).astype(jnp.bfloat16)
    d_keys = jnp.concatenate(
        [fold_heads(product(rows_of(d_low, s), rows_of(query, s), INNER)) for s in every], axis=0
    ).astype(jnp.bfloat16)
    d_values = jnp.concatenate(
        [fold_heads(product(rows_of(probs_low, s), rows_of(d_attn, s), INNER)) for s in every],
        axis=0,
    ).astype(jnp.bfloat16)

    d_query_ref[...] = product(x, d_query, INNER)
    d_key_ref[...] = product(x, d_keys, INNER)
    d_value_ref[...] = product(x, d_values, INNER)
    d_gate_ref[...] = product(x, d_glog, INNER)
    d_out_ref[...] = product(weighted, grad, INNER)

    pick_shape = (sequences, tokens)
    pick = one_where(iota(pick_shape, 1) == iota(pick_shape, 0) * residues + me)
    update_ref[...] = product(
        product(pick, weighted).astype(jnp.bfloat16), final_ref[...]
    ).astype(jnp.bfloat16)

    d_x = product(d_query, request_ref[...], OUTER)
    d_x = d_x + product(d_keys, lookup_ref[...], OUTER)
    d_x = d_x + product(d_values, content_ref[...], OUTER)
    d_x = d_x + product(d_glog, switch_ref[...], OUTER)
    d_gain_ref[...] = jnp.sum(d_x * hat, axis=0, keepdims=True)
    d_msa = standardise_features_adjoint(d_x, hat, inv, gain).astype(jnp.bfloat16)
    adjoint_ref[...] = product(pick, d_msa).astype(jnp.bfloat16)

    d_bias = jnp.sum(d_scores.reshape(sequences, residues, columns), axis=0)
    d_bias = jnp.where(
        same_key,
        jnp.broadcast_to(d_bias[:, None, :], (residues, residues, columns)).reshape(pair_shape),
        0.0,
    )
    d_pln = split_product(d_bias, headterm_wide, OUTER)
    d_headterm = split_product(pair_ln, d_bias, INNER, split_left=False)
    d_headterm_ref[...] = jnp.sum(
        d_headterm.T.reshape(HEAD_NUMBER, residues, pair_lanes), axis=1
    )
    d_pair_gain_ref[...] = jnp.sum(d_pln * pair_hat, axis=0, keepdims=True)
    pair_rows_ref[...] = (
        standardise_features_adjoint(d_pln, pair_hat, pair_inv, pair_gain)
        .astype(jnp.bfloat16)
        .reshape(residues, residues, pair_lanes)
    )
    pair_adjoint_ref[...] = pair_rows_ref[me]


def on_device_whole_part(
    alignment_embedding,
    alignment_existing_flags,
    couple_embedding,
    alignment_scaling_factor,
    couple_scaling_factor,
    request_matrix,
    lookup_matrix,
    content_matrix,
    switch_matrix,
    final_projection_matrix,
    couple_to_headterm_matrix,
    increment_adjoint,
):
    sequences, _, channels = alignment_embedding.shape
    _, residues, pair_channels = couple_embedding.shape
    devices = lax.axis_size("dap")
    vmem = pl.BlockSpec(memory_space=pltpu.VMEM)
    gathered = pl.pallas_call(
        lambda *refs: gather_kernel(devices, *refs),
        out_shape=jax.ShapeDtypeStruct((devices, 3 * sequences, channels), jnp.bfloat16),
        in_specs=[vmem] * 4,
        out_specs=vmem,
        scratch_shapes=[
            pltpu.SemaphoreType.DMA((devices - 1,)),
            pltpu.SemaphoreType.DMA((devices,)),
        ],
        compiler_params=pltpu.CompilerParams(collective_id=0, has_side_effects=True),
        name="gather_part",
    )(
        alignment_embedding.reshape(sequences, channels),
        alignment_existing_flags,
        couple_embedding.reshape(residues, pair_channels),
        increment_adjoint.reshape(sequences, channels),
    )
    span = HEAD_NUMBER * HEAD_DIMENSION
    weight = jax.ShapeDtypeStruct((channels, span), jnp.float32)
    outs = pl.pallas_call(
        part_kernel,
        out_shape=(
            jax.ShapeDtypeStruct((sequences, channels), jnp.bfloat16),
            jax.ShapeDtypeStruct((sequences, channels), jnp.bfloat16),
            jax.ShapeDtypeStruct((residues, pair_channels), jnp.bfloat16),
            weight,
            weight,
            weight,
            weight,
            jax.ShapeDtypeStruct((span, channels), jnp.float32),
            jax.ShapeDtypeStruct((HEAD_NUMBER, pair_channels), jnp.float32),
            jax.ShapeDtypeStruct((1, channels), jnp.float32),
            jax.ShapeDtypeStruct((1, pair_channels), jnp.float32),
        ),
        in_specs=[vmem] * 9,
        out_specs=(vmem,) * 11,
        scratch_shapes=[pltpu.VMEM((residues, residues, pair_channels), jnp.bfloat16)],
        compiler_params=pltpu.CompilerParams(vmem_limit_bytes=32 * 1024 * 1024),
        name="whole_part",
    )(
        gathered,
        alignment_scaling_factor.reshape(1, channels),
        couple_scaling_factor.reshape(1, pair_channels),
        request_matrix,
        lookup_matrix,
        content_matrix,
        switch_matrix,
        final_projection_matrix,
        couple_to_headterm_matrix,
    )
    return (
        outs[0].reshape(alignment_embedding.shape),
        outs[1].reshape(alignment_embedding.shape),
        outs[2].reshape(couple_embedding.shape),
        *outs[3:8],
        outs[8].T,
        outs[9].reshape(channels),
        outs[10].reshape(pair_channels),
    )


def on_device(
    alignment_embedding,
    alignment_existing_flags,
    couple_embedding,
    alignment_scaling_factor,
    couple_scaling_factor,
    request_matrix,
    lookup_matrix,
    content_matrix,
    switch_matrix,
    final_projection_matrix,
    couple_to_headterm_matrix,
    increment_adjoint,
):
    if whole_part_fits(alignment_embedding, couple_embedding):
        return on_device_whole_part(
            alignment_embedding,
            alignment_existing_flags,
            couple_embedding,
            alignment_scaling_factor,
            couple_scaling_factor,
            request_matrix,
            lookup_matrix,
            content_matrix,
            switch_matrix,
            final_projection_matrix,
            couple_to_headterm_matrix,
            increment_adjoint,
        )
    filter_shared = alignment_existing_flags.astype(jnp.bfloat16)
    alignment_line_embedding, alignment_line_flags = (
        lax.all_to_all(alignment_embedding, "dap", split_axis=0, concat_axis=1, tiled=True),
        lax.all_to_all(filter_shared, "dap", split_axis=0, concat_axis=1, tiled=True),
    )
    pair_hat, pair_inv, pair_scaled = standardise_features(
        couple_embedding.astype(jnp.float32), couple_scaling_factor
    )
    pair_ln = pair_scaled.astype(jnp.bfloat16)
    bias_rows = jnp.einsum(
        "ijc,ch->ihj", pair_ln, couple_to_headterm_matrix, preferred_element_type=jnp.float32
    ).astype(jnp.bfloat16)
    couple_headwise_terms = lax.all_gather(bias_rows, "dap", axis=0, tiled=True)

    def onward_loop_step(carry, loop_elements):
        alignment_increment, kept_intermediates = onward_one_line(
            loop_elements[0],
            loop_elements[1],
            couple_headwise_terms,
            alignment_scaling_factor,
            request_matrix,
            lookup_matrix,
            content_matrix,
            switch_matrix,
            final_projection_matrix,
        )
        return (carry, (alignment_increment, kept_intermediates))

    unused_value, (row_updates, all_saved_residuals) = lax.scan(
        onward_loop_step, None, (alignment_line_embedding, alignment_line_flags)
    )
    update_out = lax.all_to_all(row_updates, "dap", split_axis=1, concat_axis=0, tiled=True)
    seq_grad = lax.all_to_all(increment_adjoint, "dap", split_axis=0, concat_axis=1, tiled=True)
    amino_positions = alignment_line_embedding.shape[1]
    span_length = HEAD_NUMBER * HEAD_DIMENSION
    blank_matrix = (
        jnp.zeros((ALIGN_FEATURES, span_length), jnp.float32),
        jnp.zeros((ALIGN_FEATURES, span_length), jnp.float32),
        jnp.zeros((ALIGN_FEATURES, span_length), jnp.float32),
        jnp.zeros((ALIGN_FEATURES, span_length), jnp.float32),
        jnp.zeros((span_length, ALIGN_FEATURES), jnp.float32),
        jnp.zeros((ALIGN_FEATURES,), jnp.float32),
    )

    def backward_step(carry, loop_elements):
        bias_sum, subtotal_list = carry
        line_adjoint, affinity_adjoint, matrix_adjoints = reverse_one_line(
            loop_elements[0],
            loop_elements[1],
            alignment_scaling_factor,
            request_matrix,
            lookup_matrix,
            content_matrix,
            switch_matrix,
            final_projection_matrix,
        )
        subtotal_list = tuple((a + b for a, b in zip(subtotal_list, matrix_adjoints)))
        return ((bias_sum + affinity_adjoint, subtotal_list), line_adjoint)

    beginning_shift = (
        jnp.zeros((amino_positions, HEAD_NUMBER, amino_positions), jnp.float32),
        blank_matrix,
    )
    (bias_term, subtotal_list), line_adjoint_list = lax.scan(
        backward_step, beginning_shift, (seq_grad, all_saved_residuals)
    )
    additive_term_adjoint = lax.psum_scatter(bias_term, "dap", scatter_dimension=0, tiled=True)
    d_pln = jnp.einsum(
        "ihj,ch->ijc",
        additive_term_adjoint,
        couple_to_headterm_matrix.astype(jnp.float32),
        precision=lax.Precision.HIGHEST,
    )
    w_bias_part = jnp.einsum(
        "ijc,ihj->ch",
        pair_ln.astype(jnp.float32),
        additive_term_adjoint,
        precision=lax.Precision.HIGHEST,
    )
    pair_gain_part = jnp.sum(d_pln * pair_hat, axis=(0, 1))
    couple_adjoint = standardise_features_adjoint(
        d_pln, pair_hat, pair_inv, couple_scaling_factor
    ).astype(jnp.bfloat16)
    totals = lax.psum(
        (
            subtotal_list[0],
            subtotal_list[1],
            subtotal_list[2],
            subtotal_list[3],
            subtotal_list[4],
            w_bias_part,
            subtotal_list[5],
            pair_gain_part,
        ),
        "dap",
    )
    alignment_adjoint = lax.all_to_all(
        line_adjoint_list, "dap", split_axis=1, concat_axis=0, tiled=True
    )
    return (
        update_out,
        alignment_adjoint,
        couple_adjoint,
        totals[0],
        totals[1],
        totals[2],
        totals[3],
        totals[4],
        totals[5],
        totals[6],
        totals[7],
    )


def solution(mesh):
    in_specs = (
        P("dp", "dap", None),
        P("dp", "dap"),
        P(("dp", "dap"), None, None),
        P(),
        P(),
        P(),
        P(),
        P(),
        P(),
        P(),
        P(),
        P("dp", "dap", None),
    )
    out_specs = (
        P("dp", "dap", None),
        P("dp", "dap", None),
        P(("dp", "dap"), None, None),
        P("dp", None),
        P("dp", None),
        P("dp", None),
        P("dp", None),
        P("dp", None),
        P("dp", None),
        P("dp"),
        P("dp"),
    )
    return jax.shard_map(
        on_device, mesh=mesh, in_specs=in_specs, out_specs=out_specs, check_vma=False
    )
```

```python
import jax
import jax.numpy as jnp
from jax import lax
from jax.experimental import pallas as pl
from jax.experimental.pallas import tpu as pltpu
from jax.sharding import PartitionSpec as P

ALIGN_FEATURES = 256
HEAD_NUMBER = 8
HEAD_DIMENSION = 32


EPS = 1e-05


def standardise_features(value, gain):
    mean = jnp.mean(value, axis=-1, keepdims=True)
    centered = value - mean
    variance = jnp.mean(centered * centered, axis=-1, keepdims=True)
    reciprocal_spread = lax.rsqrt(variance + EPS)
    standardised_lines = centered * reciprocal_spread
    return (standardised_lines, reciprocal_spread, standardised_lines * gain)


def standardise_features_adjoint(upstream_gradient, standardised_lines, reciprocal_spread, gain):
    rescaled_request = upstream_gradient * gain
    return reciprocal_spread * (
        rescaled_request
        - jnp.mean(rescaled_request, axis=-1, keepdims=True)
        - standardised_lines
        * jnp.mean(rescaled_request * standardised_lines, axis=-1, keepdims=True)
    )


def tensor_product(left, right):
    return lax.dot_general(
        left, right, (((0,), (0,)), ((), ())), preferred_element_type=jnp.float32
    )


def onward_one_line(
    alignment_line_content,
    line_filter_flags,
    couple_headwise_terms,
    alignment_scaling_factor,
    request_matrix,
    lookup_matrix,
    content_matrix,
    switch_matrix,
    final_projection_matrix,
):
    element_number = alignment_line_content.shape[0]
    standardised_lines, reciprocal_spread, rescaled_request = standardise_features(
        alignment_line_content.astype(jnp.float32), alignment_scaling_factor
    )
    input_arrays = rescaled_request.astype(jnp.bfloat16)
    query = (
        jnp.dot(input_arrays, request_matrix, preferred_element_type=jnp.float32)
        * HEAD_DIMENSION ** (-0.5)
    ).astype(jnp.bfloat16)
    keys = jnp.dot(input_arrays, lookup_matrix, preferred_element_type=jnp.float32).astype(
        jnp.bfloat16
    )
    values = jnp.dot(input_arrays, content_matrix, preferred_element_type=jnp.float32).astype(
        jnp.bfloat16
    )
    gate_sigmoid = jax.nn.sigmoid(
        jnp.dot(input_arrays, switch_matrix, preferred_element_type=jnp.float32)
    )
    query = query.reshape(element_number, HEAD_NUMBER, HEAD_DIMENSION)
    keys = keys.reshape(element_number, HEAD_NUMBER, HEAD_DIMENSION)
    values = values.reshape(element_number, HEAD_NUMBER, HEAD_DIMENSION)
    scores = jnp.einsum("ihd,jhd->ihj", query, keys, preferred_element_type=jnp.float32)
    scores = (
        scores
        + couple_headwise_terms.astype(jnp.float32)
        + (1000000000.0 * (line_filter_flags.astype(jnp.float32) - 1.0))[None, None, :]
    )
    probs = jax.nn.softmax(scores, axis=-1)
    probs_low = probs.astype(jnp.bfloat16)
    attention_probs = jnp.einsum(
        "ihj,jhd->ihd", probs_low, values, preferred_element_type=jnp.float32
    ).reshape(element_number, HEAD_NUMBER * HEAD_DIMENSION)
    weighted_values = (gate_sigmoid * attention_probs).astype(jnp.bfloat16)
    alignment_increment = jnp.dot(
        weighted_values, final_projection_matrix, preferred_element_type=jnp.float32
    ).astype(jnp.bfloat16)
    kept_intermediates = (
        standardised_lines,
        reciprocal_spread,
        input_arrays,
        query,
        keys,
        values,
        gate_sigmoid,
        attention_probs,
        weighted_values,
        probs,
    )
    return (alignment_increment, kept_intermediates)


def reverse_one_line(
    line_adjoint_routine,
    kept_intermediates,
    alignment_scaling_factor,
    request_matrix,
    lookup_matrix,
    content_matrix,
    switch_matrix,
    final_projection_matrix,
):
    (
        standardised_lines,
        reciprocal_spread,
        input_arrays,
        query,
        keys,
        values,
        gate_sigmoid,
        attention_probs,
        weighted_values,
        probs,
    ) = kept_intermediates
    element_number = line_adjoint_routine.shape[0]
    probs_low = probs.astype(jnp.bfloat16)
    upstream_gradient = lax.dot_general(
        line_adjoint_routine,
        final_projection_matrix,
        (((1,), (1,)), ((), ())),
        preferred_element_type=jnp.float32,
    )
    d_attn = (upstream_gradient * gate_sigmoid).astype(jnp.bfloat16)
    gate_logit_gradient = (
        upstream_gradient * attention_probs * gate_sigmoid * (1.0 - gate_sigmoid)
    ).astype(jnp.bfloat16)
    d_attn_heads = d_attn.reshape(element_number, HEAD_NUMBER, HEAD_DIMENSION)
    d_probs = jnp.einsum("ihd,jhd->ihj", d_attn_heads, values, preferred_element_type=jnp.float32)
    affinity_adjoint = probs * (d_probs - jnp.sum(probs * d_probs, axis=-1, keepdims=True))
    d_low = affinity_adjoint.astype(jnp.bfloat16)
    query_gradient = (
        (
            jnp.einsum("ihj,jhd->ihd", d_low, keys, preferred_element_type=jnp.float32)
            * HEAD_DIMENSION ** (-0.5)
        )
        .astype(jnp.bfloat16)
        .reshape(element_number, HEAD_NUMBER * HEAD_DIMENSION)
    )
    key_gradient = (
        jnp.einsum("ihj,ihd->jhd", d_low, query, preferred_element_type=jnp.float32)
        .astype(jnp.bfloat16)
        .reshape(element_number, HEAD_NUMBER * HEAD_DIMENSION)
    )
    value_gradient = (
        jnp.einsum("ihj,ihd->jhd", probs_low, d_attn_heads, preferred_element_type=jnp.float32)
        .astype(jnp.bfloat16)
        .reshape(element_number, HEAD_NUMBER * HEAD_DIMENSION)
    )
    backward_result = (((1,), (1,)), ((), ()))
    argument_adjoints = lax.dot_general(
        query_gradient, request_matrix, backward_result, preferred_element_type=jnp.float32
    )
    argument_adjoints = argument_adjoints + lax.dot_general(
        key_gradient, lookup_matrix, backward_result, preferred_element_type=jnp.float32
    )
    argument_adjoints = argument_adjoints + lax.dot_general(
        value_gradient, content_matrix, backward_result, preferred_element_type=jnp.float32
    )
    argument_adjoints = argument_adjoints + lax.dot_general(
        gate_logit_gradient, switch_matrix, backward_result, preferred_element_type=jnp.float32
    )
    line_adjoint = standardise_features_adjoint(
        argument_adjoints, standardised_lines, reciprocal_spread, alignment_scaling_factor
    ).astype(jnp.bfloat16)
    matrix_adjoints = (
        tensor_product(input_arrays, query_gradient),
        tensor_product(input_arrays, key_gradient),
        tensor_product(input_arrays, value_gradient),
        tensor_product(input_arrays, gate_logit_gradient),
        tensor_product(weighted_values, line_adjoint_routine),
        jnp.sum(argument_adjoints * standardised_lines, axis=0),
    )
    return (line_adjoint, affinity_adjoint, matrix_adjoints)


LANES = 128
ROW_TILE = 16


def whole_part_fits(alignment_embedding, couple_embedding):
    sequences, owned, _ = alignment_embedding.shape
    owned_pairs, residues, pair_channels = couple_embedding.shape
    devices = lax.axis_size("dap")
    return (
        owned == 1
        and owned_pairs == 1
        and devices == residues
        and devices % 4 == 0
        and HEAD_NUMBER * residues == LANES
        and pair_channels == LANES
        and sequences == residues
        and sequences % ROW_TILE == 0
    )


def gather_kernel(devices, msa_ref, flag_ref, pair_ref, grad_ref, all_ref, send_sem, recv_sem):
    me = lax.axis_index("dap")
    rows = msa_ref.shape[0]
    lanes = pair_ref.shape[1]
    planes = devices // 4
    core = lax.rem(me, 2)
    row = lax.rem(me // 2, 2)
    sibling = me + 1 - 2 * core
    across = me + 2 - 4 * row
    far = [lax.rem(me + 4 * k, devices) for k in range(1, planes)]
    far_across = [lax.rem(across + 4 * k, devices) for k in range(1, planes)]

    barrier = pltpu.get_barrier_semaphore()
    for peer in far + [across, sibling]:
        pl.semaphore_signal(
            barrier, inc=1, device_id={"dap": peer}, device_id_type=pl.DeviceIdType.MESH
        )
    all_ref[me, 0:rows, :] = msa_ref[...]
    all_ref[me, rows : 2 * rows, :] = grad_ref[...]
    all_ref[me, 2 * rows :, 0:lanes] = pair_ref[...]
    flags = jnp.broadcast_to(flag_ref[...].astype(jnp.float32), (rows, rows))
    all_ref[me, 2 * rows :, lanes:] = jnp.concatenate(
        [flags, jnp.zeros((rows, lanes - rows), jnp.float32)], axis=1
    ).astype(jnp.bfloat16)
    pl.semaphore_wait(barrier, planes + 1)

    sent = []

    def send(slot, peer):
        copy = pltpu.make_async_remote_copy(
            src_ref=all_ref.at[slot],
            dst_ref=all_ref.at[slot],
            send_sem=send_sem.at[len(sent)],
            recv_sem=recv_sem.at[slot],
            device_id={"dap": peer},
            device_id_type=pl.DeviceIdType.MESH,
        )
        copy.start()
        sent.append(copy)

    def arrive(slot):
        pltpu.make_async_remote_copy(
            src_ref=all_ref.at[slot],
            dst_ref=all_ref.at[slot],
            send_sem=send_sem.at[0],
            recv_sem=recv_sem.at[slot],
            device_id={"dap": sibling},
            device_id_type=pl.DeviceIdType.MESH,
        ).wait_recv()

    for peer in far:
        send(me, peer)
    send(me, across)
    send(me, sibling)
    arrive(across)
    send(across, sibling)
    for slot in far:
        arrive(slot)
        send(slot, across)
        send(slot, sibling)
    for slot in far_across:
        arrive(slot)
        send(slot, sibling)
    sibling_across = sibling + 2 - 4 * row
    for k in range(planes):
        arrive(lax.rem(sibling + 4 * k, devices))
        arrive(lax.rem(sibling_across + 4 * k, devices))
    for copy in sent:
        copy.wait_send()


def iota(shape, dimension):
    return lax.broadcasted_iota(jnp.int32, shape, dimension)


def one_where(condition):
    return jnp.where(condition, 1.0, 0.0).astype(jnp.bfloat16)


def product(left, right, contract=((1,), (0,))):
    return lax.dot_general(left, right, (contract, ((), ())), preferred_element_type=jnp.float32)


OUTER = ((1,), (1,))
INNER = ((0,), (0,))


def split_product(left, right, contract=((1,), (0,)), split_left=True):
    wide = left if split_left else right
    upper = wide.astype(jnp.bfloat16)
    lower = (wide - upper.astype(jnp.float32)).astype(jnp.bfloat16)
    if split_left:
        return product(upper, right, contract) + product(lower, right, contract)
    return product(left, upper, contract) + product(left, lower, contract)


def over_group(value, width, combine):
    lane = iota(value.shape, 1)
    size = value.shape[1]
    step = 1
    while step < width:
        other = jnp.where(
            (lane // step) % 2 == 0,
            pltpu.roll(value, size - step, 1),
            pltpu.roll(value, step, 1),
        )
        value = combine(value, other)
        step *= 2
    return value


def part_kernel(
    all_ref,
    gain_ref,
    pair_gain_ref,
    request_ref,
    lookup_ref,
    content_ref,
    switch_ref,
    final_ref,
    headterm_ref,
    update_ref,
    adjoint_ref,
    pair_adjoint_ref,
    d_query_ref,
    d_key_ref,
    d_value_ref,
    d_gate_ref,
    d_out_ref,
    d_headterm_ref,
    d_gain_ref,
    d_pair_gain_ref,
    pair_rows_ref,
):
    me = lax.axis_index("dap")
    residues = all_ref.shape[0]
    sequences = all_ref.shape[1] // 3
    channels = all_ref.shape[2]
    tokens = residues * sequences
    span = HEAD_NUMBER * HEAD_DIMENSION
    columns = HEAD_NUMBER * residues
    gain = gain_ref[...]
    pair_gain = pair_gain_ref[...]

    pair_lanes = pair_gain.shape[1]
    pair_raw = all_ref[:, 2 * sequences :, 0:pair_lanes].reshape(residues * residues, pair_lanes)
    pair_hat, pair_inv, pair_scaled = standardise_features(
        pair_raw.astype(jnp.float32), pair_gain
    )
    pair_ln = pair_scaled.astype(jnp.bfloat16)
    spread = one_where(
        iota((HEAD_NUMBER, columns), 0) == iota((HEAD_NUMBER, columns), 1) // residues
    )
    headterm_wide = product(headterm_ref[...], spread, INNER).astype(jnp.bfloat16)
    pair_shape = (residues * residues, columns)
    same_key = iota(pair_shape, 0) % residues == iota(pair_shape, 1) % residues
    bias = jnp.sum(
        jnp.where(same_key, product(pair_ln, headterm_wide), 0.0).reshape(
            residues, residues, columns
        ),
        axis=1,
    )
    bias = bias.astype(jnp.bfloat16).astype(jnp.float32)

    flags = all_ref[:, 2 * sequences :, pair_lanes:].astype(jnp.float32)
    flags = flags[:, 0, :].astype(jnp.bfloat16)
    key_shape = (residues, columns)
    flags = product(flags, one_where(iota(key_shape, 0) == iota(key_shape, 1) % residues), INNER)
    fill = 1000000000.0 * (flags[0:sequences] - 1.0)

    square = (tokens, tokens)
    reorder = one_where(
        (iota(square, 0) // residues == iota(square, 1) % sequences)
        & (iota(square, 0) % residues == iota(square, 1) // sequences)
    )
    raw = product(reorder, all_ref[:, 0:sequences, :].reshape(tokens, channels))
    grad = product(
        reorder, all_ref[:, sequences : 2 * sequences, :].reshape(tokens, channels)
    ).astype(jnp.bfloat16)

    hat, inv, scaled = standardise_features(raw, gain)
    x = scaled.astype(jnp.bfloat16)
    query = (product(x, request_ref[...]) * HEAD_DIMENSION ** (-0.5)).astype(jnp.bfloat16)
    keys = product(x, lookup_ref[...]).astype(jnp.bfloat16)
    values = product(x, content_ref[...]).astype(jnp.bfloat16)
    gate = jax.nn.sigmoid(product(x, switch_ref[...]))
    upstream = product(grad, final_ref[...], OUTER)
    d_attn = (upstream * gate).astype(jnp.bfloat16)

    head_shape = (columns, span)
    own_head = iota(head_shape, 0) // residues == iota(head_shape, 1) // HEAD_DIMENSION
    own_head_one = one_where(own_head)

    def rows_of(value, s):
        return value[s * residues : (s + 1) * residues]

    def by_head(value):
        return jnp.concatenate([value] * HEAD_NUMBER, axis=0) * own_head_one

    def fold_heads(value):
        return jnp.sum(
            jnp.where(own_head, value, 0.0).reshape(HEAD_NUMBER, residues, span), axis=0
        )

    every = range(sequences)
    wide_keys = [by_head(rows_of(keys, s)) for s in every]
    wide_values = [by_head(rows_of(values, s)) for s in every]
    scores = jnp.concatenate(
        [
            product(rows_of(query, s), wide_keys[s], OUTER) + bias + fill[s : s + 1]
            for s in every
        ],
        axis=0,
    )
    scores = jnp.exp(scores - over_group(scores, residues, jnp.maximum))
    probs = scores / over_group(scores, residues, jnp.add)
    probs_low = probs.astype(jnp.bfloat16)
    d_probs = jnp.concatenate(
        [product(rows_of(d_attn, s), wide_values[s], OUTER) for s in every], axis=0
    )
    d_scores = probs * (d_probs - over_group(probs * d_probs, residues, jnp.add))
    d_low = d_scores.astype(jnp.bfloat16)
    attended = jnp.concatenate(
        [product(rows_of(probs_low, s), wide_values[s]) for s in every], axis=0
    )
    weighted = (gate * attended).astype(jnp.bfloat16)
    d_glog = (upstream * attended * gate * (1.0 - gate)).astype(jnp.bfloat16)
    d_query = jnp.concatenate(
        [product(rows_of(d_low, s), wide_keys[s]) for s in every], axis=0
    )
    d_query = (d_query * HEAD_DIMENSION ** (-0.5)).astype(jnp.bfloat16)
    d_keys = jnp.concatenate(
        [fold_heads(product(rows_of(d_low, s), rows_of(query, s), INNER)) for s in every], axis=0
    ).astype(jnp.bfloat16)
    d_values = jnp.concatenate(
        [fold_heads(product(rows_of(probs_low, s), rows_of(d_attn, s), INNER)) for s in every],
        axis=0,
    ).astype(jnp.bfloat16)

    d_query_ref[...] = product(x, d_query, INNER)
    d_key_ref[...] = product(x, d_keys, INNER)
    d_value_ref[...] = product(x, d_values, INNER)
    d_gate_ref[...] = product(x, d_glog, INNER)
    d_out_ref[...] = product(weighted, grad, INNER)

    pick_shape = (sequences, tokens)
    pick = one_where(iota(pick_shape, 1) == iota(pick_shape, 0) * residues + me)
    update_ref[...] = product(
        product(pick, weighted).astype(jnp.bfloat16), final_ref[...]
    ).astype(jnp.bfloat16)

    d_x = product(d_query, request_ref[...], OUTER)
    d_x = d_x + product(d_keys, lookup_ref[...], OUTER)
    d_x = d_x + product(d_values, content_ref[...], OUTER)
    d_x = d_x + product(d_glog, switch_ref[...], OUTER)
    d_gain_ref[...] = jnp.sum(d_x * hat, axis=0, keepdims=True)
    d_msa = standardise_features_adjoint(d_x, hat, inv, gain).astype(jnp.bfloat16)
    adjoint_ref[...] = product(pick, d_msa).astype(jnp.bfloat16)

    d_bias = jnp.sum(d_scores.reshape(sequences, residues, columns), axis=0)
    d_bias = jnp.where(
        same_key,
        jnp.broadcast_to(d_bias[:, None, :], (residues, residues, columns)).reshape(pair_shape),
        0.0,
    )
    d_pln = split_product(d_bias, headterm_wide, OUTER)
    d_headterm = split_product(pair_ln, d_bias, INNER, split_left=False)
    d_headterm_ref[...] = jnp.sum(
        d_headterm.T.reshape(HEAD_NUMBER, residues, pair_lanes), axis=1
    )
    d_pair_gain_ref[...] = jnp.sum(d_pln * pair_hat, axis=0, keepdims=True)
    pair_rows_ref[...] = (
        standardise_features_adjoint(d_pln, pair_hat, pair_inv, pair_gain)
        .astype(jnp.bfloat16)
        .reshape(residues, residues, pair_lanes)
    )
    pair_adjoint_ref[...] = pair_rows_ref[me]


def on_device_whole_part(
    alignment_embedding,
    alignment_existing_flags,
    couple_embedding,
    alignment_scaling_factor,
    couple_scaling_factor,
    request_matrix,
    lookup_matrix,
    content_matrix,
    switch_matrix,
    final_projection_matrix,
    couple_to_headterm_matrix,
    increment_adjoint,
):
    sequences, _, channels = alignment_embedding.shape
    _, residues, pair_channels = couple_embedding.shape
    devices = lax.axis_size("dap")
    vmem = pl.BlockSpec(memory_space=pltpu.VMEM)
    gathered = pl.pallas_call(
        lambda *refs: gather_kernel(devices, *refs),
        out_shape=jax.ShapeDtypeStruct((devices, 3 * sequences, channels), jnp.bfloat16),
        in_specs=[vmem] * 4,
        out_specs=vmem,
        scratch_shapes=[
            pltpu.SemaphoreType.DMA((devices - 1,)),
            pltpu.SemaphoreType.DMA((devices,)),
        ],
        compiler_params=pltpu.CompilerParams(
            collective_id=0, has_side_effects=True, vmem_limit_bytes=8 * 1024 * 1024
        ),
        cost_estimate=pl.CostEstimate(
            flops=0, bytes_accessed=100 * devices * 3 * sequences * channels * 2, transcendentals=0
        ),
        name="gather_part",
    )(
        alignment_embedding.reshape(sequences, channels),
        alignment_existing_flags.T,
        couple_embedding.reshape(residues, pair_channels),
        increment_adjoint.reshape(sequences, channels),
    )
    span = HEAD_NUMBER * HEAD_DIMENSION
    weight = jax.ShapeDtypeStruct((channels, span), jnp.float32)
    outs = pl.pallas_call(
        part_kernel,
        out_shape=(
            jax.ShapeDtypeStruct((sequences, channels), jnp.bfloat16),
            jax.ShapeDtypeStruct((sequences, channels), jnp.bfloat16),
            jax.ShapeDtypeStruct((residues, pair_channels), jnp.bfloat16),
            weight,
            weight,
            weight,
            weight,
            jax.ShapeDtypeStruct((span, channels), jnp.float32),
            jax.ShapeDtypeStruct((HEAD_NUMBER, pair_channels), jnp.float32),
            jax.ShapeDtypeStruct((1, channels), jnp.float32),
            jax.ShapeDtypeStruct((1, pair_channels), jnp.float32),
        ),
        in_specs=[vmem] * 9,
        out_specs=(vmem,) * 11,
        scratch_shapes=[pltpu.VMEM((residues, residues, pair_channels), jnp.bfloat16)],
        compiler_params=pltpu.CompilerParams(vmem_limit_bytes=24 * 1024 * 1024),
        name="whole_part",
    )(
        gathered,
        alignment_scaling_factor.reshape(1, channels),
        couple_scaling_factor.reshape(1, pair_channels),
        request_matrix,
        lookup_matrix,
        content_matrix,
        switch_matrix,
        final_projection_matrix,
        couple_to_headterm_matrix.T,
    )
    return (
        outs[0].reshape(alignment_embedding.shape),
        outs[1].reshape(alignment_embedding.shape),
        outs[2].reshape(couple_embedding.shape),
        *outs[3:8],
        outs[8].T,
        outs[9].reshape(channels),
        outs[10].reshape(pair_channels),
    )


def on_device(
    alignment_embedding,
    alignment_existing_flags,
    couple_embedding,
    alignment_scaling_factor,
    couple_scaling_factor,
    request_matrix,
    lookup_matrix,
    content_matrix,
    switch_matrix,
    final_projection_matrix,
    couple_to_headterm_matrix,
    increment_adjoint,
):
    if whole_part_fits(alignment_embedding, couple_embedding):
        return on_device_whole_part(
            alignment_embedding,
            alignment_existing_flags,
            couple_embedding,
            alignment_scaling_factor,
            couple_scaling_factor,
            request_matrix,
            lookup_matrix,
            content_matrix,
            switch_matrix,
            final_projection_matrix,
            couple_to_headterm_matrix,
            increment_adjoint,
        )
    filter_shared = alignment_existing_flags.astype(jnp.bfloat16)
    alignment_line_embedding, alignment_line_flags = (
        lax.all_to_all(alignment_embedding, "dap", split_axis=0, concat_axis=1, tiled=True),
        lax.all_to_all(filter_shared, "dap", split_axis=0, concat_axis=1, tiled=True),
    )
    pair_hat, pair_inv, pair_scaled = standardise_features(
        couple_embedding.astype(jnp.float32), couple_scaling_factor
    )
    pair_ln = pair_scaled.astype(jnp.bfloat16)
    bias_rows = jnp.einsum(
        "ijc,ch->ihj", pair_ln, couple_to_headterm_matrix, preferred_element_type=jnp.float32
    ).astype(jnp.bfloat16)
    couple_headwise_terms = lax.all_gather(bias_rows, "dap", axis=0, tiled=True)

    def onward_loop_step(carry, loop_elements):
        alignment_increment, kept_intermediates = onward_one_line(
            loop_elements[0],
            loop_elements[1],
            couple_headwise_terms,
            alignment_scaling_factor,
            request_matrix,
            lookup_matrix,
            content_matrix,
            switch_matrix,
            final_projection_matrix,
        )
        return (carry, (alignment_increment, kept_intermediates))

    unused_value, (row_updates, all_saved_residuals) = lax.scan(
        onward_loop_step, None, (alignment_line_embedding, alignment_line_flags)
    )
    update_out = lax.all_to_all(row_updates, "dap", split_axis=1, concat_axis=0, tiled=True)
    seq_grad = lax.all_to_all(increment_adjoint, "dap", split_axis=0, concat_axis=1, tiled=True)
    amino_positions = alignment_line_embedding.shape[1]
    span_length = HEAD_NUMBER * HEAD_DIMENSION
    blank_matrix = (
        jnp.zeros((ALIGN_FEATURES, span_length), jnp.float32),
        jnp.zeros((ALIGN_FEATURES, span_length), jnp.float32),
        jnp.zeros((ALIGN_FEATURES, span_length), jnp.float32),
        jnp.zeros((ALIGN_FEATURES, span_length), jnp.float32),
        jnp.zeros((span_length, ALIGN_FEATURES), jnp.float32),
        jnp.zeros((ALIGN_FEATURES,), jnp.float32),
    )

    def backward_step(carry, loop_elements):
        bias_sum, subtotal_list = carry
        line_adjoint, affinity_adjoint, matrix_adjoints = reverse_one_line(
            loop_elements[0],
            loop_elements[1],
            alignment_scaling_factor,
            request_matrix,
            lookup_matrix,
            content_matrix,
            switch_matrix,
            final_projection_matrix,
        )
        subtotal_list = tuple((a + b for a, b in zip(subtotal_list, matrix_adjoints)))
        return ((bias_sum + affinity_adjoint, subtotal_list), line_adjoint)

    beginning_shift = (
        jnp.zeros((amino_positions, HEAD_NUMBER, amino_positions), jnp.float32),
        blank_matrix,
    )
    (bias_term, subtotal_list), line_adjoint_list = lax.scan(
        backward_step, beginning_shift, (seq_grad, all_saved_residuals)
    )
    additive_term_adjoint = lax.psum_scatter(bias_term, "dap", scatter_dimension=0, tiled=True)
    d_pln = jnp.einsum(
        "ihj,ch->ijc",
        additive_term_adjoint,
        couple_to_headterm_matrix.astype(jnp.float32),
        precision=lax.Precision.HIGHEST,
    )
    w_bias_part = jnp.einsum(
        "ijc,ihj->ch",
        pair_ln.astype(jnp.float32),
        additive_term_adjoint,
        precision=lax.Precision.HIGHEST,
    )
    pair_gain_part = jnp.sum(d_pln * pair_hat, axis=(0, 1))
    couple_adjoint = standardise_features_adjoint(
        d_pln, pair_hat, pair_inv, couple_scaling_factor
    ).astype(jnp.bfloat16)
    totals = lax.psum(
        (
            subtotal_list[0],
            subtotal_list[1],
            subtotal_list[2],
            subtotal_list[3],
            subtotal_list[4],
            w_bias_part,
            subtotal_list[5],
            pair_gain_part,
        ),
        "dap",
    )
    alignment_adjoint = lax.all_to_all(
        line_adjoint_list, "dap", split_axis=1, concat_axis=0, tiled=True
    )
    return (
        update_out,
        alignment_adjoint,
        couple_adjoint,
        totals[0],
        totals[1],
        totals[2],
        totals[3],
        totals[4],
        totals[5],
        totals[6],
        totals[7],
    )


def solution(mesh):
    in_specs = (
        P("dp", "dap", None),
        P("dp", "dap"),
        P(("dp", "dap"), None, None),
        P(),
        P(),
        P(),
        P(),
        P(),
        P(),
        P(),
        P(),
        P("dp", "dap", None),
    )
    out_specs = (
        P("dp", "dap", None),
        P("dp", "dap", None),
        P(("dp", "dap"), None, None),
        P("dp", None),
        P("dp", None),
        P("dp", None),
        P("dp", None),
        P("dp", None),
        P("dp", None),
        P("dp"),
        P("dp"),
    )
    return jax.shard_map(
        on_device, mesh=mesh, in_specs=in_specs, out_specs=out_specs, check_vma=False
    )
```

```python
import jax
import jax.numpy as jnp
from jax import lax
from jax.experimental import pallas as pl
from jax.experimental.pallas import tpu as pltpu
from jax.sharding import PartitionSpec as P

ALIGN_FEATURES = 256
HEAD_NUMBER = 8
HEAD_DIMENSION = 32


EPS = 1e-05


def standardise_features(value, gain):
    mean = jnp.mean(value, axis=-1, keepdims=True)
    centered = value - mean
    variance = jnp.mean(centered * centered, axis=-1, keepdims=True)
    reciprocal_spread = lax.rsqrt(variance + EPS)
    standardised_lines = centered * reciprocal_spread
    return (standardised_lines, reciprocal_spread, standardised_lines * gain)


def standardise_features_adjoint(upstream_gradient, standardised_lines, reciprocal_spread, gain):
    rescaled_request = upstream_gradient * gain
    return reciprocal_spread * (
        rescaled_request
        - jnp.mean(rescaled_request, axis=-1, keepdims=True)
        - standardised_lines
        * jnp.mean(rescaled_request * standardised_lines, axis=-1, keepdims=True)
    )


def tensor_product(left, right):
    return lax.dot_general(
        left, right, (((0,), (0,)), ((), ())), preferred_element_type=jnp.float32
    )


def onward_one_line(
    alignment_line_content,
    line_filter_flags,
    couple_headwise_terms,
    alignment_scaling_factor,
    request_matrix,
    lookup_matrix,
    content_matrix,
    switch_matrix,
    final_projection_matrix,
):
    element_number = alignment_line_content.shape[0]
    standardised_lines, reciprocal_spread, rescaled_request = standardise_features(
        alignment_line_content.astype(jnp.float32), alignment_scaling_factor
    )
    input_arrays = rescaled_request.astype(jnp.bfloat16)
    query = (
        jnp.dot(input_arrays, request_matrix, preferred_element_type=jnp.float32)
        * HEAD_DIMENSION ** (-0.5)
    ).astype(jnp.bfloat16)
    keys = jnp.dot(input_arrays, lookup_matrix, preferred_element_type=jnp.float32).astype(
        jnp.bfloat16
    )
    values = jnp.dot(input_arrays, content_matrix, preferred_element_type=jnp.float32).astype(
        jnp.bfloat16
    )
    gate_sigmoid = jax.nn.sigmoid(
        jnp.dot(input_arrays, switch_matrix, preferred_element_type=jnp.float32)
    )
    query = query.reshape(element_number, HEAD_NUMBER, HEAD_DIMENSION)
    keys = keys.reshape(element_number, HEAD_NUMBER, HEAD_DIMENSION)
    values = values.reshape(element_number, HEAD_NUMBER, HEAD_DIMENSION)
    scores = jnp.einsum("ihd,jhd->ihj", query, keys, preferred_element_type=jnp.float32)
    scores = (
        scores
        + couple_headwise_terms.astype(jnp.float32)
        + (1000000000.0 * (line_filter_flags.astype(jnp.float32) - 1.0))[None, None, :]
    )
    probs = jax.nn.softmax(scores, axis=-1)
    probs_low = probs.astype(jnp.bfloat16)
    attention_probs = jnp.einsum(
        "ihj,jhd->ihd", probs_low, values, preferred_element_type=jnp.float32
    ).reshape(element_number, HEAD_NUMBER * HEAD_DIMENSION)
    weighted_values = (gate_sigmoid * attention_probs).astype(jnp.bfloat16)
    alignment_increment = jnp.dot(
        weighted_values, final_projection_matrix, preferred_element_type=jnp.float32
    ).astype(jnp.bfloat16)
    kept_intermediates = (
        standardised_lines,
        reciprocal_spread,
        input_arrays,
        query,
        keys,
        values,
        gate_sigmoid,
        attention_probs,
        weighted_values,
        probs,
    )
    return (alignment_increment, kept_intermediates)


def reverse_one_line(
    line_adjoint_routine,
    kept_intermediates,
    alignment_scaling_factor,
    request_matrix,
    lookup_matrix,
    content_matrix,
    switch_matrix,
    final_projection_matrix,
):
    (
        standardised_lines,
        reciprocal_spread,
        input_arrays,
        query,
        keys,
        values,
        gate_sigmoid,
        attention_probs,
        weighted_values,
        probs,
    ) = kept_intermediates
    element_number = line_adjoint_routine.shape[0]
    probs_low = probs.astype(jnp.bfloat16)
    upstream_gradient = lax.dot_general(
        line_adjoint_routine,
        final_projection_matrix,
        (((1,), (1,)), ((), ())),
        preferred_element_type=jnp.float32,
    )
    d_attn = (upstream_gradient * gate_sigmoid).astype(jnp.bfloat16)
    gate_logit_gradient = (
        upstream_gradient * attention_probs * gate_sigmoid * (1.0 - gate_sigmoid)
    ).astype(jnp.bfloat16)
    d_attn_heads = d_attn.reshape(element_number, HEAD_NUMBER, HEAD_DIMENSION)
    d_probs = jnp.einsum("ihd,jhd->ihj", d_attn_heads, values, preferred_element_type=jnp.float32)
    affinity_adjoint = probs * (d_probs - jnp.sum(probs * d_probs, axis=-1, keepdims=True))
    d_low = affinity_adjoint.astype(jnp.bfloat16)
    query_gradient = (
        (
            jnp.einsum("ihj,jhd->ihd", d_low, keys, preferred_element_type=jnp.float32)
            * HEAD_DIMENSION ** (-0.5)
        )
        .astype(jnp.bfloat16)
        .reshape(element_number, HEAD_NUMBER * HEAD_DIMENSION)
    )
    key_gradient = (
        jnp.einsum("ihj,ihd->jhd", d_low, query, preferred_element_type=jnp.float32)
        .astype(jnp.bfloat16)
        .reshape(element_number, HEAD_NUMBER * HEAD_DIMENSION)
    )
    value_gradient = (
        jnp.einsum("ihj,ihd->jhd", probs_low, d_attn_heads, preferred_element_type=jnp.float32)
        .astype(jnp.bfloat16)
        .reshape(element_number, HEAD_NUMBER * HEAD_DIMENSION)
    )
    backward_result = (((1,), (1,)), ((), ()))
    argument_adjoints = lax.dot_general(
        query_gradient, request_matrix, backward_result, preferred_element_type=jnp.float32
    )
    argument_adjoints = argument_adjoints + lax.dot_general(
        key_gradient, lookup_matrix, backward_result, preferred_element_type=jnp.float32
    )
    argument_adjoints = argument_adjoints + lax.dot_general(
        value_gradient, content_matrix, backward_result, preferred_element_type=jnp.float32
    )
    argument_adjoints = argument_adjoints + lax.dot_general(
        gate_logit_gradient, switch_matrix, backward_result, preferred_element_type=jnp.float32
    )
    line_adjoint = standardise_features_adjoint(
        argument_adjoints, standardised_lines, reciprocal_spread, alignment_scaling_factor
    ).astype(jnp.bfloat16)
    matrix_adjoints = (
        tensor_product(input_arrays, query_gradient),
        tensor_product(input_arrays, key_gradient),
        tensor_product(input_arrays, value_gradient),
        tensor_product(input_arrays, gate_logit_gradient),
        tensor_product(weighted_values, line_adjoint_routine),
        jnp.sum(argument_adjoints * standardised_lines, axis=0),
    )
    return (line_adjoint, affinity_adjoint, matrix_adjoints)


LANES = 128
ROW_TILE = 16


def whole_part_fits(alignment_embedding, couple_embedding):
    sequences, owned, _ = alignment_embedding.shape
    owned_pairs, residues, pair_channels = couple_embedding.shape
    devices = lax.axis_size("dap")
    return (
        owned == 1
        and owned_pairs == 1
        and devices == residues
        and devices % 4 == 0
        and HEAD_NUMBER * residues == LANES
        and pair_channels == LANES
        and sequences == residues
        and sequences % ROW_TILE == 0
    )


def gather_kernel(devices, block_ref, all_ref, send_sem, recv_sem):
    me = lax.axis_index("dap")
    planes = devices // 4
    place = lax.rem(me, 4)
    core = lax.rem(place, 2)
    row = place // 2
    sibling = me + 1 - 2 * core
    across = me + 2 - 4 * row
    opposite = me + 3 - 2 * place
    beside = [across, opposite, sibling]
    far = [lax.rem(me + 4 * k, devices) for k in range(1, planes)]

    barrier = pltpu.get_barrier_semaphore()
    for peer in far + beside:
        pl.semaphore_signal(
            barrier, inc=1, device_id={"dap": peer}, device_id_type=pl.DeviceIdType.MESH
        )
    all_ref[me] = block_ref[...]
    pl.semaphore_wait(barrier, planes + 2)

    sent = []

    def send(slot, peer):
        copy = pltpu.make_async_remote_copy(
            src_ref=all_ref.at[slot],
            dst_ref=all_ref.at[slot],
            send_sem=send_sem.at[len(sent)],
            recv_sem=recv_sem.at[slot],
            device_id={"dap": peer},
            device_id_type=pl.DeviceIdType.MESH,
        )
        copy.start()
        sent.append(copy)

    def arrive(slot):
        pltpu.make_async_remote_copy(
            src_ref=all_ref.at[slot],
            dst_ref=all_ref.at[slot],
            send_sem=send_sem.at[0],
            recv_sem=recv_sem.at[slot],
            device_id={"dap": sibling},
            device_id_type=pl.DeviceIdType.MESH,
        ).wait_recv()

    for peer in far + beside:
        send(me, peer)
    for slot in far:
        arrive(slot)
        for peer in beside:
            send(slot, peer)
    for first in beside:
        for k in range(planes):
            arrive(lax.rem(first + 4 * k, devices))
    for copy in sent:
        copy.wait_send()


def iota(shape, dimension):
    return lax.broadcasted_iota(jnp.int32, shape, dimension)


def one_where(condition):
    return jnp.where(condition, 1.0, 0.0).astype(jnp.bfloat16)


def product(left, right, contract=((1,), (0,))):
    return lax.dot_general(left, right, (contract, ((), ())), preferred_element_type=jnp.float32)


OUTER = ((1,), (1,))
INNER = ((0,), (0,))


def split_product(left, right, contract=((1,), (0,)), split_left=True):
    wide = left if split_left else right
    upper = wide.astype(jnp.bfloat16)
    lower = (wide - upper.astype(jnp.float32)).astype(jnp.bfloat16)
    if split_left:
        return product(upper, right, contract) + product(lower, right, contract)
    return product(left, upper, contract) + product(left, lower, contract)


def over_group(value, width, combine):
    lane = iota(value.shape, 1)
    size = value.shape[1]
    step = 1
    while step < width:
        other = jnp.where(
            (lane // step) % 2 == 0,
            pltpu.roll(value, size - step, 1),
            pltpu.roll(value, step, 1),
        )
        value = combine(value, other)
        step *= 2
    return value


def part_kernel(
    all_ref,
    gain_ref,
    pair_gain_ref,
    request_ref,
    lookup_ref,
    content_ref,
    switch_ref,
    final_ref,
    headterm_ref,
    update_ref,
    adjoint_ref,
    pair_adjoint_ref,
    d_query_ref,
    d_key_ref,
    d_value_ref,
    d_gate_ref,
    d_out_ref,
    d_headterm_ref,
    d_gain_ref,
    d_pair_gain_ref,
    pair_rows_ref,
):
    me = lax.axis_index("dap")
    residues = all_ref.shape[0]
    sequences = all_ref.shape[1] // 3
    channels = all_ref.shape[2]
    tokens = residues * sequences
    span = HEAD_NUMBER * HEAD_DIMENSION
    columns = HEAD_NUMBER * residues
    gain = gain_ref[...]
    pair_gain = pair_gain_ref[...]

    pair_lanes = pair_gain.shape[1]
    pair_raw = all_ref[:, 2 * sequences :, 0:pair_lanes].reshape(residues * residues, pair_lanes)
    pair_hat, pair_inv, pair_scaled = standardise_features(
        pair_raw.astype(jnp.float32), pair_gain
    )
    pair_ln = pair_scaled.astype(jnp.bfloat16)
    spread = one_where(
        iota((HEAD_NUMBER, columns), 0) == iota((HEAD_NUMBER, columns), 1) // residues
    )
    headterm_wide = product(headterm_ref[...], spread, INNER).astype(jnp.bfloat16)
    pair_shape = (residues * residues, columns)
    same_key = iota(pair_shape, 0) % residues == iota(pair_shape, 1) % residues
    bias = jnp.sum(
        jnp.where(same_key, product(pair_ln, headterm_wide), 0.0).reshape(
            residues, residues, columns
        ),
        axis=1,
    )
    bias = bias.astype(jnp.bfloat16).astype(jnp.float32)

    flags = all_ref[:, 2 * sequences :, pair_lanes:].astype(jnp.float32)
    flags = flags[:, 0, :].astype(jnp.bfloat16)
    key_shape = (residues, columns)
    flags = product(flags, one_where(iota(key_shape, 0) == iota(key_shape, 1) % residues), INNER)
    fill = 1000000000.0 * (flags[0:sequences] - 1.0)

    square = (tokens, tokens)
    reorder = one_where(
        (iota(square, 0) // residues == iota(square, 1) % sequences)
        & (iota(square, 0) % residues == iota(square, 1) // sequences)
    )
    raw = product(reorder, all_ref[:, 0:sequences, :].reshape(tokens, channels))
    grad = product(
        reorder, all_ref[:, sequences : 2 * sequences, :].reshape(tokens, channels)
    ).astype(jnp.bfloat16)

    hat, inv, scaled = standardise_features(raw, gain)
    x = scaled.astype(jnp.bfloat16)
    query = (product(x, request_ref[...]) * HEAD_DIMENSION ** (-0.5)).astype(jnp.bfloat16)
    keys = product(x, lookup_ref[...]).astype(jnp.bfloat16)
    values = product(x, content_ref[...]).astype(jnp.bfloat16)
    gate = jax.nn.sigmoid(product(x, switch_ref[...]))
    upstream = product(grad, final_ref[...], OUTER)
    d_attn = (upstream * gate).astype(jnp.bfloat16)

    head_shape = (columns, span)
    own_head = iota(head_shape, 0) // residues == iota(head_shape, 1) // HEAD_DIMENSION
    own_head_one = one_where(own_head)

    def rows_of(value, s):
        return value[s * residues : (s + 1) * residues]

    def by_head(value):
        return jnp.concatenate([value] * HEAD_NUMBER, axis=0) * own_head_one

    def fold_heads(value):
        return jnp.sum(
            jnp.where(own_head, value, 0.0).reshape(HEAD_NUMBER, residues, span), axis=0
        )

    every = range(sequences)
    wide_keys = [by_head(rows_of(keys, s)) for s in every]
    wide_values = [by_head(rows_of(values, s)) for s in every]
    scores = jnp.concatenate(
        [
            product(rows_of(query, s), wide_keys[s], OUTER) + bias + fill[s : s + 1]
            for s in every
        ],
        axis=0,
    )
    scores = jnp.exp(scores - over_group(scores, residues, jnp.maximum))
    probs = scores / over_group(scores, residues, jnp.add)
    probs_low = probs.astype(jnp.bfloat16)
    d_probs = jnp.concatenate(
        [product(rows_of(d_attn, s), wide_values[s], OUTER) for s in every], axis=0
    )
    d_scores = probs * (d_probs - over_group(probs * d_probs, residues, jnp.add))
    d_low = d_scores.astype(jnp.bfloat16)
    attended = jnp.concatenate(
        [product(rows_of(probs_low, s), wide_values[s]) for s in every], axis=0
    )
    weighted = (gate * attended).astype(jnp.bfloat16)
    d_glog = (upstream * attended * gate * (1.0 - gate)).astype(jnp.bfloat16)
    d_query = jnp.concatenate(
        [product(rows_of(d_low, s), wide_keys[s]) for s in every], axis=0
    )
    d_query = (d_query * HEAD_DIMENSION ** (-0.5)).astype(jnp.bfloat16)
    d_keys = jnp.concatenate(
        [fold_heads(product(rows_of(d_low, s), rows_of(query, s), INNER)) for s in every], axis=0
    ).astype(jnp.bfloat16)
    d_values = jnp.concatenate(
        [fold_heads(product(rows_of(probs_low, s), rows_of(d_attn, s), INNER)) for s in every],
        axis=0,
    ).astype(jnp.bfloat16)

    d_query_ref[...] = product(x, d_query, INNER)
    d_key_ref[...] = product(x, d_keys, INNER)
    d_value_ref[...] = product(x, d_values, INNER)
    d_gate_ref[...] = product(x, d_glog, INNER)
    d_out_ref[...] = product(weighted, grad, INNER)

    pick_shape = (sequences, tokens)
    pick = one_where(iota(pick_shape, 1) == iota(pick_shape, 0) * residues + me)
    update_ref[...] = product(
        product(pick, weighted).astype(jnp.bfloat16), final_ref[...]
    ).astype(jnp.bfloat16)

    d_x = product(d_query, request_ref[...], OUTER)
    d_x = d_x + product(d_keys, lookup_ref[...], OUTER)
    d_x = d_x + product(d_values, content_ref[...], OUTER)
    d_x = d_x + product(d_glog, switch_ref[...], OUTER)
    d_gain_ref[...] = jnp.sum(d_x * hat, axis=0, keepdims=True)
    d_msa = standardise_features_adjoint(d_x, hat, inv, gain).astype(jnp.bfloat16)
    adjoint_ref[...] = product(pick, d_msa).astype(jnp.bfloat16)

    d_bias = jnp.sum(d_scores.reshape(sequences, residues, columns), axis=0)
    d_bias = jnp.where(
        same_key,
        jnp.broadcast_to(d_bias[:, None, :], (residues, residues, columns)).reshape(pair_shape),
        0.0,
    )
    d_pln = split_product(d_bias, headterm_wide, OUTER)
    d_headterm = split_product(pair_ln, d_bias, INNER, split_left=False)
    d_headterm_ref[...] = jnp.sum(
        d_headterm.T.reshape(HEAD_NUMBER, residues, pair_lanes), axis=1
    )
    d_pair_gain_ref[...] = jnp.sum(d_pln * pair_hat, axis=0, keepdims=True)
    pair_rows_ref[...] = (
        standardise_features_adjoint(d_pln, pair_hat, pair_inv, pair_gain)
        .astype(jnp.bfloat16)
        .reshape(residues, residues, pair_lanes)
    )
    pair_adjoint_ref[...] = pair_rows_ref[me]


def on_device_whole_part(
    alignment_embedding,
    alignment_existing_flags,
    couple_embedding,
    alignment_scaling_factor,
    couple_scaling_factor,
    request_matrix,
    lookup_matrix,
    content_matrix,
    switch_matrix,
    final_projection_matrix,
    couple_to_headterm_matrix,
    increment_adjoint,
):
    sequences, _, channels = alignment_embedding.shape
    _, residues, pair_channels = couple_embedding.shape
    devices = lax.axis_size("dap")
    vmem = pl.BlockSpec(memory_space=pltpu.VMEM)
    flags = jnp.pad(
        alignment_existing_flags.T.astype(jnp.bfloat16),
        ((0, 0), (0, channels - pair_channels - sequences)),
    )
    block = jnp.concatenate(
        [
            alignment_embedding.reshape(sequences, channels),
            increment_adjoint.reshape(sequences, channels),
            jnp.concatenate(
                [
                    couple_embedding.reshape(residues, pair_channels),
                    jnp.broadcast_to(flags, (residues, channels - pair_channels)),
                ],
                axis=1,
            ),
        ],
        axis=0,
    )
    gathered = pl.pallas_call(
        lambda *refs: gather_kernel(devices, *refs),
        out_shape=jax.ShapeDtypeStruct((devices, *block.shape), jnp.bfloat16),
        in_specs=[vmem],
        out_specs=vmem,
        scratch_shapes=[
            pltpu.SemaphoreType.DMA((devices - 1,)),
            pltpu.SemaphoreType.DMA((devices,)),
        ],
        compiler_params=pltpu.CompilerParams(
            collective_id=0, has_side_effects=True, vmem_limit_bytes=8 * 1024 * 1024
        ),
        cost_estimate=pl.CostEstimate(
            flops=0, bytes_accessed=100 * devices * block.size * 2, transcendentals=0
        ),
        name="gather_part",
    )(block)
    span = HEAD_NUMBER * HEAD_DIMENSION
    weight = jax.ShapeDtypeStruct((channels, span), jnp.float32)
    outs = pl.pallas_call(
        part_kernel,
        out_shape=(
            jax.ShapeDtypeStruct((sequences, channels), jnp.bfloat16),
            jax.ShapeDtypeStruct((sequences, channels), jnp.bfloat16),
            jax.ShapeDtypeStruct((residues, pair_channels), jnp.bfloat16),
            weight,
            weight,
            weight,
            weight,
            jax.ShapeDtypeStruct((span, channels), jnp.float32),
            jax.ShapeDtypeStruct((HEAD_NUMBER, pair_channels), jnp.float32),
            jax.ShapeDtypeStruct((1, channels), jnp.float32),
            jax.ShapeDtypeStruct((1, pair_channels), jnp.float32),
        ),
        in_specs=[vmem] * 9,
        out_specs=(vmem,) * 11,
        scratch_shapes=[pltpu.VMEM((residues, residues, pair_channels), jnp.bfloat16)],
        compiler_params=pltpu.CompilerParams(vmem_limit_bytes=24 * 1024 * 1024),
        name="whole_part",
    )(
        gathered,
        alignment_scaling_factor.reshape(1, channels),
        couple_scaling_factor.reshape(1, pair_channels),
        request_matrix,
        lookup_matrix,
        content_matrix,
        switch_matrix,
        final_projection_matrix,
        couple_to_headterm_matrix.T,
    )
    return (
        outs[0].reshape(alignment_embedding.shape),
        outs[1].reshape(alignment_embedding.shape),
        outs[2].reshape(couple_embedding.shape),
        *outs[3:8],
        outs[8].T,
        outs[9].reshape(channels),
        outs[10].reshape(pair_channels),
    )


def on_device(
    alignment_embedding,
    alignment_existing_flags,
    couple_embedding,
    alignment_scaling_factor,
    couple_scaling_factor,
    request_matrix,
    lookup_matrix,
    content_matrix,
    switch_matrix,
    final_projection_matrix,
    couple_to_headterm_matrix,
    increment_adjoint,
):
    if whole_part_fits(alignment_embedding, couple_embedding):
        return on_device_whole_part(
            alignment_embedding,
            alignment_existing_flags,
            couple_embedding,
            alignment_scaling_factor,
            couple_scaling_factor,
            request_matrix,
            lookup_matrix,
            content_matrix,
            switch_matrix,
            final_projection_matrix,
            couple_to_headterm_matrix,
            increment_adjoint,
        )
    filter_shared = alignment_existing_flags.astype(jnp.bfloat16)
    alignment_line_embedding, alignment_line_flags = (
        lax.all_to_all(alignment_embedding, "dap", split_axis=0, concat_axis=1, tiled=True),
        lax.all_to_all(filter_shared, "dap", split_axis=0, concat_axis=1, tiled=True),
    )
    pair_hat, pair_inv, pair_scaled = standardise_features(
        couple_embedding.astype(jnp.float32), couple_scaling_factor
    )
    pair_ln = pair_scaled.astype(jnp.bfloat16)
    bias_rows = jnp.einsum(
        "ijc,ch->ihj", pair_ln, couple_to_headterm_matrix, preferred_element_type=jnp.float32
    ).astype(jnp.bfloat16)
    couple_headwise_terms = lax.all_gather(bias_rows, "dap", axis=0, tiled=True)

    def onward_loop_step(carry, loop_elements):
        alignment_increment, kept_intermediates = onward_one_line(
            loop_elements[0],
            loop_elements[1],
            couple_headwise_terms,
            alignment_scaling_factor,
            request_matrix,
            lookup_matrix,
            content_matrix,
            switch_matrix,
            final_projection_matrix,
        )
        return (carry, (alignment_increment, kept_intermediates))

    unused_value, (row_updates, all_saved_residuals) = lax.scan(
        onward_loop_step, None, (alignment_line_embedding, alignment_line_flags)
    )
    update_out = lax.all_to_all(row_updates, "dap", split_axis=1, concat_axis=0, tiled=True)
    seq_grad = lax.all_to_all(increment_adjoint, "dap", split_axis=0, concat_axis=1, tiled=True)
    amino_positions = alignment_line_embedding.shape[1]
    span_length = HEAD_NUMBER * HEAD_DIMENSION
    blank_matrix = (
        jnp.zeros((ALIGN_FEATURES, span_length), jnp.float32),
        jnp.zeros((ALIGN_FEATURES, span_length), jnp.float32),
        jnp.zeros((ALIGN_FEATURES, span_length), jnp.float32),
        jnp.zeros((ALIGN_FEATURES, span_length), jnp.float32),
        jnp.zeros((span_length, ALIGN_FEATURES), jnp.float32),
        jnp.zeros((ALIGN_FEATURES,), jnp.float32),
    )

    def backward_step(carry, loop_elements):
        bias_sum, subtotal_list = carry
        line_adjoint, affinity_adjoint, matrix_adjoints = reverse_one_line(
            loop_elements[0],
            loop_elements[1],
            alignment_scaling_factor,
            request_matrix,
            lookup_matrix,
            content_matrix,
            switch_matrix,
            final_projection_matrix,
        )
        subtotal_list = tuple((a + b for a, b in zip(subtotal_list, matrix_adjoints)))
        return ((bias_sum + affinity_adjoint, subtotal_list), line_adjoint)

    beginning_shift = (
        jnp.zeros((amino_positions, HEAD_NUMBER, amino_positions), jnp.float32),
        blank_matrix,
    )
    (bias_term, subtotal_list), line_adjoint_list = lax.scan(
        backward_step, beginning_shift, (seq_grad, all_saved_residuals)
    )
    additive_term_adjoint = lax.psum_scatter(bias_term, "dap", scatter_dimension=0, tiled=True)
    d_pln = jnp.einsum(
        "ihj,ch->ijc",
        additive_term_adjoint,
        couple_to_headterm_matrix.astype(jnp.float32),
        precision=lax.Precision.HIGHEST,
    )
    w_bias_part = jnp.einsum(
        "ijc,ihj->ch",
        pair_ln.astype(jnp.float32),
        additive_term_adjoint,
        precision=lax.Precision.HIGHEST,
    )
    pair_gain_part = jnp.sum(d_pln * pair_hat, axis=(0, 1))
    couple_adjoint = standardise_features_adjoint(
        d_pln, pair_hat, pair_inv, couple_scaling_factor
    ).astype(jnp.bfloat16)
    totals = lax.psum(
        (
            subtotal_list[0],
            subtotal_list[1],
            subtotal_list[2],
            subtotal_list[3],
            subtotal_list[4],
            w_bias_part,
            subtotal_list[5],
            pair_gain_part,
        ),
        "dap",
    )
    alignment_adjoint = lax.all_to_all(
        line_adjoint_list, "dap", split_axis=1, concat_axis=0, tiled=True
    )
    return (
        update_out,
        alignment_adjoint,
        couple_adjoint,
        totals[0],
        totals[1],
        totals[2],
        totals[3],
        totals[4],
        totals[5],
        totals[6],
        totals[7],
    )


def solution(mesh):
    in_specs = (
        P("dp", "dap", None),
        P("dp", "dap"),
        P(("dp", "dap"), None, None),
        P(),
        P(),
        P(),
        P(),
        P(),
        P(),
        P(),
        P(),
        P("dp", "dap", None),
    )
    out_specs = (
        P("dp", "dap", None),
        P("dp", "dap", None),
        P(("dp", "dap"), None, None),
        P("dp", None),
        P("dp", None),
        P("dp", None),
        P("dp", None),
        P("dp", None),
        P("dp", None),
        P("dp"),
        P("dp"),
    )
    return jax.shard_map(
        on_device, mesh=mesh, in_specs=in_specs, out_specs=out_specs, check_vma=False
    )
```

```python
import jax
import jax.numpy as jnp
from jax import lax
from jax.experimental import pallas as pl
from jax.experimental.pallas import tpu as pltpu
from jax.sharding import PartitionSpec as P

ALIGN_FEATURES = 256
HEAD_NUMBER = 8
HEAD_DIMENSION = 32


EPS = 1e-05


def standardise_features(value, gain):
    mean = jnp.mean(value, axis=-1, keepdims=True)
    centered = value - mean
    variance = jnp.mean(centered * centered, axis=-1, keepdims=True)
    reciprocal_spread = lax.rsqrt(variance + EPS)
    standardised_lines = centered * reciprocal_spread
    return (standardised_lines, reciprocal_spread, standardised_lines * gain)


def standardise_features_adjoint(upstream_gradient, standardised_lines, reciprocal_spread, gain):
    rescaled_request = upstream_gradient * gain
    return reciprocal_spread * (
        rescaled_request
        - jnp.mean(rescaled_request, axis=-1, keepdims=True)
        - standardised_lines
        * jnp.mean(rescaled_request * standardised_lines, axis=-1, keepdims=True)
    )


def tensor_product(left, right):
    return lax.dot_general(
        left, right, (((0,), (0,)), ((), ())), preferred_element_type=jnp.float32
    )


def onward_one_line(
    alignment_line_content,
    line_filter_flags,
    couple_headwise_terms,
    alignment_scaling_factor,
    request_matrix,
    lookup_matrix,
    content_matrix,
    switch_matrix,
    final_projection_matrix,
):
    element_number = alignment_line_content.shape[0]
    standardised_lines, reciprocal_spread, rescaled_request = standardise_features(
        alignment_line_content.astype(jnp.float32), alignment_scaling_factor
    )
    input_arrays = rescaled_request.astype(jnp.bfloat16)
    query = (
        jnp.dot(input_arrays, request_matrix, preferred_element_type=jnp.float32)
        * HEAD_DIMENSION ** (-0.5)
    ).astype(jnp.bfloat16)
    keys = jnp.dot(input_arrays, lookup_matrix, preferred_element_type=jnp.float32).astype(
        jnp.bfloat16
    )
    values = jnp.dot(input_arrays, content_matrix, preferred_element_type=jnp.float32).astype(
        jnp.bfloat16
    )
    gate_sigmoid = jax.nn.sigmoid(
        jnp.dot(input_arrays, switch_matrix, preferred_element_type=jnp.float32)
    )
    query = query.reshape(element_number, HEAD_NUMBER, HEAD_DIMENSION)
    keys = keys.reshape(element_number, HEAD_NUMBER, HEAD_DIMENSION)
    values = values.reshape(element_number, HEAD_NUMBER, HEAD_DIMENSION)
    scores = jnp.einsum("ihd,jhd->ihj", query, keys, preferred_element_type=jnp.float32)
    scores = (
        scores
        + couple_headwise_terms.astype(jnp.float32)
        + (1000000000.0 * (line_filter_flags.astype(jnp.float32) - 1.0))[None, None, :]
    )
    probs = jax.nn.softmax(scores, axis=-1)
    probs_low = probs.astype(jnp.bfloat16)
    attention_probs = jnp.einsum(
        "ihj,jhd->ihd", probs_low, values, preferred_element_type=jnp.float32
    ).reshape(element_number, HEAD_NUMBER * HEAD_DIMENSION)
    weighted_values = (gate_sigmoid * attention_probs).astype(jnp.bfloat16)
    alignment_increment = jnp.dot(
        weighted_values, final_projection_matrix, preferred_element_type=jnp.float32
    ).astype(jnp.bfloat16)
    kept_intermediates = (
        standardised_lines,
        reciprocal_spread,
        input_arrays,
        query,
        keys,
        values,
        gate_sigmoid,
        attention_probs,
        weighted_values,
        probs,
    )
    return (alignment_increment, kept_intermediates)


def reverse_one_line(
    line_adjoint_routine,
    kept_intermediates,
    alignment_scaling_factor,
    request_matrix,
    lookup_matrix,
    content_matrix,
    switch_matrix,
    final_projection_matrix,
):
    (
        standardised_lines,
        reciprocal_spread,
        input_arrays,
        query,
        keys,
        values,
        gate_sigmoid,
        attention_probs,
        weighted_values,
        probs,
    ) = kept_intermediates
    element_number = line_adjoint_routine.shape[0]
    probs_low = probs.astype(jnp.bfloat16)
    upstream_gradient = lax.dot_general(
        line_adjoint_routine,
        final_projection_matrix,
        (((1,), (1,)), ((), ())),
        preferred_element_type=jnp.float32,
    )
    d_attn = (upstream_gradient * gate_sigmoid).astype(jnp.bfloat16)
    gate_logit_gradient = (
        upstream_gradient * attention_probs * gate_sigmoid * (1.0 - gate_sigmoid)
    ).astype(jnp.bfloat16)
    d_attn_heads = d_attn.reshape(element_number, HEAD_NUMBER, HEAD_DIMENSION)
    d_probs = jnp.einsum("ihd,jhd->ihj", d_attn_heads, values, preferred_element_type=jnp.float32)
    affinity_adjoint = probs * (d_probs - jnp.sum(probs * d_probs, axis=-1, keepdims=True))
    d_low = affinity_adjoint.astype(jnp.bfloat16)
    query_gradient = (
        (
            jnp.einsum("ihj,jhd->ihd", d_low, keys, preferred_element_type=jnp.float32)
            * HEAD_DIMENSION ** (-0.5)
        )
        .astype(jnp.bfloat16)
        .reshape(element_number, HEAD_NUMBER * HEAD_DIMENSION)
    )
    key_gradient = (
        jnp.einsum("ihj,ihd->jhd", d_low, query, preferred_element_type=jnp.float32)
        .astype(jnp.bfloat16)
        .reshape(element_number, HEAD_NUMBER * HEAD_DIMENSION)
    )
    value_gradient = (
        jnp.einsum("ihj,ihd->jhd", probs_low, d_attn_heads, preferred_element_type=jnp.float32)
        .astype(jnp.bfloat16)
        .reshape(element_number, HEAD_NUMBER * HEAD_DIMENSION)
    )
    backward_result = (((1,), (1,)), ((), ()))
    argument_adjoints = lax.dot_general(
        query_gradient, request_matrix, backward_result, preferred_element_type=jnp.float32
    )
    argument_adjoints = argument_adjoints + lax.dot_general(
        key_gradient, lookup_matrix, backward_result, preferred_element_type=jnp.float32
    )
    argument_adjoints = argument_adjoints + lax.dot_general(
        value_gradient, content_matrix, backward_result, preferred_element_type=jnp.float32
    )
    argument_adjoints = argument_adjoints + lax.dot_general(
        gate_logit_gradient, switch_matrix, backward_result, preferred_element_type=jnp.float32
    )
    line_adjoint = standardise_features_adjoint(
        argument_adjoints, standardised_lines, reciprocal_spread, alignment_scaling_factor
    ).astype(jnp.bfloat16)
    matrix_adjoints = (
        tensor_product(input_arrays, query_gradient),
        tensor_product(input_arrays, key_gradient),
        tensor_product(input_arrays, value_gradient),
        tensor_product(input_arrays, gate_logit_gradient),
        tensor_product(weighted_values, line_adjoint_routine),
        jnp.sum(argument_adjoints * standardised_lines, axis=0),
    )
    return (line_adjoint, affinity_adjoint, matrix_adjoints)


LANES = 128
ROW_TILE = 16


def whole_part_fits(alignment_embedding, couple_embedding):
    sequences, owned, _ = alignment_embedding.shape
    owned_pairs, residues, pair_channels = couple_embedding.shape
    devices = lax.axis_size("dap")
    return (
        owned == 1
        and owned_pairs == 1
        and devices == residues
        and devices % 8 == 0
        and HEAD_NUMBER * residues == LANES
        and pair_channels == LANES
        and sequences == residues
        and sequences % ROW_TILE == 0
    )


def gather_kernel(devices, msa_ref, grad_ref, pair_ref, all_ref, send_sem, recv_sem):
    rows = msa_ref.shape[0]
    me = lax.axis_index("dap")
    planes = devices // 4
    place = lax.rem(me, 4)
    core = lax.rem(place, 2)
    row = place // 2
    sibling = me + 1 - 2 * core
    across = me + 2 - 4 * row
    opposite = me + 3 - 2 * place
    beside = [across, opposite, sibling]
    far = [lax.rem(me + 4 * k, devices) for k in range(1, planes)]
    far_across = [lax.rem(across + 4 * k, devices) for k in range(1, planes)]
    direct = far + far_across[0::2]

    barrier = pltpu.get_barrier_semaphore()
    for peer in direct + beside:
        pl.semaphore_signal(
            barrier, inc=1, device_id={"dap": peer}, device_id_type=pl.DeviceIdType.MESH
        )
    all_ref[me, 0:rows, :] = msa_ref[...]
    all_ref[me, rows : 2 * rows, :] = grad_ref[...]
    all_ref[me, 2 * rows :, :] = pair_ref[...]
    pl.semaphore_wait(barrier, len(direct) + len(beside))

    sent = []

    def send(slot, peer):
        copy = pltpu.make_async_remote_copy(
            src_ref=all_ref.at[slot],
            dst_ref=all_ref.at[slot],
            send_sem=send_sem.at[len(sent)],
            recv_sem=recv_sem.at[slot],
            device_id={"dap": peer},
            device_id_type=pl.DeviceIdType.MESH,
        )
        copy.start()
        sent.append(copy)

    def arrive(slot):
        pltpu.make_async_remote_copy(
            src_ref=all_ref.at[slot],
            dst_ref=all_ref.at[slot],
            send_sem=send_sem.at[0],
            recv_sem=recv_sem.at[slot],
            device_id={"dap": sibling},
            device_id_type=pl.DeviceIdType.MESH,
        ).wait_recv()

    for peer in far[1::2] + [across, opposite] + far[0::2] + far_across[0::2] + [sibling]:
        send(me, peer)
    for slot in far[1::2]:
        arrive(slot)
        for peer in beside:
            send(slot, peer)
    for slot in far[0::2] + far_across[0::2]:
        arrive(slot)
        send(slot, sibling)
    for slot in [across, opposite] + far_across[1::2]:
        arrive(slot)
    for k in range(planes):
        arrive(lax.rem(sibling + 4 * k, devices))
    for k in range(1, planes):
        arrive(lax.rem(opposite + 4 * k, devices))
    for copy in sent:
        copy.wait_send()


def iota(shape, dimension):
    return lax.broadcasted_iota(jnp.int32, shape, dimension)


def one_where(condition):
    return jnp.where(condition, 1.0, 0.0).astype(jnp.bfloat16)


def product(left, right, contract=((1,), (0,))):
    return lax.dot_general(left, right, (contract, ((), ())), preferred_element_type=jnp.float32)


OUTER = ((1,), (1,))
INNER = ((0,), (0,))


def split_product(left, right, contract=((1,), (0,)), split_left=True):
    wide = left if split_left else right
    upper = wide.astype(jnp.bfloat16)
    lower = (wide - upper.astype(jnp.float32)).astype(jnp.bfloat16)
    if split_left:
        return product(upper, right, contract) + product(lower, right, contract)
    return product(left, upper, contract) + product(left, lower, contract)


def over_group(value, width, combine):
    lane = iota(value.shape, 1)
    size = value.shape[1]
    step = 1
    while step < width:
        other = jnp.where(
            (lane // step) % 2 == 0,
            pltpu.roll(value, size - step, 1),
            pltpu.roll(value, step, 1),
        )
        value = combine(value, other)
        step *= 2
    return value


def part_kernel(
    all_ref,
    gain_ref,
    pair_gain_ref,
    request_ref,
    lookup_ref,
    content_ref,
    tail_ref,
    headterm_ref,
    update_ref,
    adjoint_ref,
    pair_adjoint_ref,
    d_query_ref,
    d_key_ref,
    d_value_ref,
    d_gate_ref,
    d_out_ref,
    d_headterm_ref,
    d_gain_ref,
    d_pair_gain_ref,
    pair_rows_ref,
):
    me = lax.axis_index("dap")
    residues = all_ref.shape[0]
    sequences = all_ref.shape[1] // 3
    channels = all_ref.shape[2]
    tokens = residues * sequences
    span = HEAD_NUMBER * HEAD_DIMENSION
    columns = HEAD_NUMBER * residues
    gain = gain_ref[...]
    pair_gain = pair_gain_ref[...]

    pair_lanes = pair_gain.shape[1]
    pair_raw = all_ref[:, 2 * sequences :, 0:pair_lanes].reshape(residues * residues, pair_lanes)
    pair_hat, pair_inv, pair_scaled = standardise_features(
        pair_raw.astype(jnp.float32), pair_gain
    )
    pair_ln = pair_scaled.astype(jnp.bfloat16)
    spread = one_where(
        iota((HEAD_NUMBER, columns), 0) == iota((HEAD_NUMBER, columns), 1) // residues
    )
    headterm_wide = product(headterm_ref[...], spread, INNER).astype(jnp.bfloat16)
    pair_shape = (residues * residues, columns)
    same_key = iota(pair_shape, 0) % residues == iota(pair_shape, 1) % residues
    bias = jnp.sum(
        jnp.where(same_key, product(pair_ln, headterm_wide), 0.0).reshape(
            residues, residues, columns
        ),
        axis=1,
    )
    bias = bias.astype(jnp.bfloat16).astype(jnp.float32)

    flags = all_ref[:, 2 * sequences :, pair_lanes:].astype(jnp.float32)
    flags = flags[:, 0, :].astype(jnp.bfloat16)
    key_shape = (residues, columns)
    flags = product(flags, one_where(iota(key_shape, 0) == iota(key_shape, 1) % residues), INNER)
    fill = 1000000000.0 * (flags[0:sequences] - 1.0)

    square = (tokens, tokens)
    reorder = one_where(
        (iota(square, 0) // residues == iota(square, 1) % sequences)
        & (iota(square, 0) % residues == iota(square, 1) // sequences)
    )
    raw = product(reorder, all_ref[:, 0:sequences, :].reshape(tokens, channels))
    grad = product(
        reorder, all_ref[:, sequences : 2 * sequences, :].reshape(tokens, channels)
    ).astype(jnp.bfloat16)

    hat, inv, scaled = standardise_features(raw, gain)
    x = scaled.astype(jnp.bfloat16)
    query = (product(x, request_ref[...]) * HEAD_DIMENSION ** (-0.5)).astype(jnp.bfloat16)
    keys = product(x, lookup_ref[...]).astype(jnp.bfloat16)
    values = product(x, content_ref[...]).astype(jnp.bfloat16)
    gate = jax.nn.sigmoid(product(x, tail_ref[0:channels, :]))
    upstream = product(grad, tail_ref[channels:, :], OUTER)
    d_attn = (upstream * gate).astype(jnp.bfloat16)

    head_shape = (columns, span)
    own_head = iota(head_shape, 0) // residues == iota(head_shape, 1) // HEAD_DIMENSION
    own_head_one = one_where(own_head)

    def rows_of(value, s):
        return value[s * residues : (s + 1) * residues]

    def by_head(value):
        return jnp.concatenate([value] * HEAD_NUMBER, axis=0) * own_head_one

    def fold_heads(value):
        return jnp.sum(
            jnp.where(own_head, value, 0.0).reshape(HEAD_NUMBER, residues, span), axis=0
        )

    every = range(sequences)
    wide_keys = [by_head(rows_of(keys, s)) for s in every]
    wide_values = [by_head(rows_of(values, s)) for s in every]
    scores = jnp.concatenate(
        [
            product(rows_of(query, s), wide_keys[s], OUTER) + bias + fill[s : s + 1]
            for s in every
        ],
        axis=0,
    )
    scores = jnp.exp(scores - over_group(scores, residues, jnp.maximum))
    probs = scores / over_group(scores, residues, jnp.add)
    probs_low = probs.astype(jnp.bfloat16)
    d_probs = jnp.concatenate(
        [product(rows_of(d_attn, s), wide_values[s], OUTER) for s in every], axis=0
    )
    d_scores = probs * (d_probs - over_group(probs * d_probs, residues, jnp.add))
    d_low = d_scores.astype(jnp.bfloat16)
    attended = jnp.concatenate(
        [product(rows_of(probs_low, s), wide_values[s]) for s in every], axis=0
    )
    weighted = (gate * attended).astype(jnp.bfloat16)
    d_glog = (upstream * attended * gate * (1.0 - gate)).astype(jnp.bfloat16)
    d_query = jnp.concatenate(
        [product(rows_of(d_low, s), wide_keys[s]) for s in every], axis=0
    )
    d_query = (d_query * HEAD_DIMENSION ** (-0.5)).astype(jnp.bfloat16)
    d_keys = jnp.concatenate(
        [fold_heads(product(rows_of(d_low, s), rows_of(query, s), INNER)) for s in every], axis=0
    ).astype(jnp.bfloat16)
    d_values = jnp.concatenate(
        [fold_heads(product(rows_of(probs_low, s), rows_of(d_attn, s), INNER)) for s in every],
        axis=0,
    ).astype(jnp.bfloat16)

    d_query_ref[...] = product(x, d_query, INNER)
    d_key_ref[...] = product(x, d_keys, INNER)
    d_value_ref[...] = product(x, d_values, INNER)
    d_gate_ref[...] = product(x, d_glog, INNER)
    d_out_ref[...] = product(weighted, grad, INNER)

    pick_shape = (sequences, tokens)
    pick = one_where(iota(pick_shape, 1) == iota(pick_shape, 0) * residues + me)
    update_ref[...] = product(
        product(pick, weighted).astype(jnp.bfloat16), tail_ref[channels:, :]
    ).astype(jnp.bfloat16)

    d_x = product(d_query, request_ref[...], OUTER)
    d_x = d_x + product(d_keys, lookup_ref[...], OUTER)
    d_x = d_x + product(d_values, content_ref[...], OUTER)
    d_x = d_x + product(d_glog, tail_ref[0:channels, :], OUTER)
    d_gain_ref[...] = jnp.sum(d_x * hat, axis=0, keepdims=True)
    d_msa = standardise_features_adjoint(d_x, hat, inv, gain).astype(jnp.bfloat16)
    adjoint_ref[...] = product(pick, d_msa).astype(jnp.bfloat16)

    d_bias = jnp.sum(d_scores.reshape(sequences, residues, columns), axis=0)
    d_bias = jnp.where(
        same_key,
        jnp.broadcast_to(d_bias[:, None, :], (residues, residues, columns)).reshape(pair_shape),
        0.0,
    )
    d_pln = split_product(d_bias, headterm_wide, OUTER)
    d_headterm = split_product(pair_ln, d_bias, INNER, split_left=False)
    d_headterm_ref[...] = jnp.sum(
        d_headterm.T.reshape(HEAD_NUMBER, residues, pair_lanes), axis=1
    )
    d_pair_gain_ref[...] = jnp.sum(d_pln * pair_hat, axis=0, keepdims=True)
    pair_rows_ref[...] = (
        standardise_features_adjoint(d_pln, pair_hat, pair_inv, pair_gain)
        .astype(jnp.bfloat16)
        .reshape(residues, residues, pair_lanes)
    )
    pair_adjoint_ref[...] = pair_rows_ref[me]


def on_device_whole_part(
    alignment_embedding,
    alignment_existing_flags,
    couple_embedding,
    alignment_scaling_factor,
    couple_scaling_factor,
    request_matrix,
    lookup_matrix,
    content_matrix,
    switch_matrix,
    final_projection_matrix,
    couple_to_headterm_matrix,
    increment_adjoint,
):
    sequences, _, channels = alignment_embedding.shape
    _, residues, pair_channels = couple_embedding.shape
    devices = lax.axis_size("dap")
    vmem = pl.BlockSpec(memory_space=pltpu.VMEM)
    flags = jnp.pad(
        alignment_existing_flags.T.astype(jnp.bfloat16),
        ((0, 0), (0, channels - pair_channels - sequences)),
    )
    pair_block = jnp.concatenate(
        [
            couple_embedding.reshape(residues, pair_channels),
            jnp.broadcast_to(flags, (residues, channels - pair_channels)),
        ],
        axis=1,
    )
    block_shape = (3 * sequences, channels)
    gathered = pl.pallas_call(
        lambda *refs: gather_kernel(devices, *refs),
        out_shape=jax.ShapeDtypeStruct((devices, *block_shape), jnp.bfloat16),
        in_specs=[vmem] * 3,
        out_specs=vmem,
        scratch_shapes=[
            pltpu.SemaphoreType.DMA((devices - 1,)),
            pltpu.SemaphoreType.DMA((devices,)),
        ],
        compiler_params=pltpu.CompilerParams(
            collective_id=0, has_side_effects=True, vmem_limit_bytes=8 * 1024 * 1024
        ),
        cost_estimate=pl.CostEstimate(
            flops=0, bytes_accessed=100 * devices * 3 * sequences * channels * 2, transcendentals=0
        ),
        name="gather_part",
    )(
        alignment_embedding.reshape(sequences, channels),
        increment_adjoint.reshape(sequences, channels),
        pair_block,
    )
    span = HEAD_NUMBER * HEAD_DIMENSION
    weight = jax.ShapeDtypeStruct((channels, span), jnp.float32)
    outs = pl.pallas_call(
        part_kernel,
        out_shape=(
            jax.ShapeDtypeStruct((sequences, channels), jnp.bfloat16),
            jax.ShapeDtypeStruct((sequences, channels), jnp.bfloat16),
            jax.ShapeDtypeStruct((residues, pair_channels), jnp.bfloat16),
            weight,
            weight,
            weight,
            weight,
            jax.ShapeDtypeStruct((span, channels), jnp.float32),
            jax.ShapeDtypeStruct((HEAD_NUMBER, pair_channels), jnp.float32),
            jax.ShapeDtypeStruct((1, channels), jnp.float32),
            jax.ShapeDtypeStruct((1, pair_channels), jnp.float32),
        ),
        in_specs=[vmem] * 8,
        out_specs=(vmem,) * 11,
        scratch_shapes=[pltpu.VMEM((residues, residues, pair_channels), jnp.bfloat16)],
        compiler_params=pltpu.CompilerParams(vmem_limit_bytes=24 * 1024 * 1024),
        name="whole_part",
    )(
        gathered,
        alignment_scaling_factor.reshape(1, channels),
        couple_scaling_factor.reshape(1, pair_channels),
        request_matrix,
        lookup_matrix,
        content_matrix,
        jnp.concatenate([switch_matrix, final_projection_matrix]),
        couple_to_headterm_matrix.T,
    )
    return (
        outs[0].reshape(alignment_embedding.shape),
        outs[1].reshape(alignment_embedding.shape),
        outs[2].reshape(couple_embedding.shape),
        *outs[3:8],
        outs[8].T,
        outs[9].reshape(channels),
        outs[10].reshape(pair_channels),
    )


def on_device(
    alignment_embedding,
    alignment_existing_flags,
    couple_embedding,
    alignment_scaling_factor,
    couple_scaling_factor,
    request_matrix,
    lookup_matrix,
    content_matrix,
    switch_matrix,
    final_projection_matrix,
    couple_to_headterm_matrix,
    increment_adjoint,
):
    if whole_part_fits(alignment_embedding, couple_embedding):
        return on_device_whole_part(
            alignment_embedding,
            alignment_existing_flags,
            couple_embedding,
            alignment_scaling_factor,
            couple_scaling_factor,
            request_matrix,
            lookup_matrix,
            content_matrix,
            switch_matrix,
            final_projection_matrix,
            couple_to_headterm_matrix,
            increment_adjoint,
        )
    filter_shared = alignment_existing_flags.astype(jnp.bfloat16)
    alignment_line_embedding, alignment_line_flags = (
        lax.all_to_all(alignment_embedding, "dap", split_axis=0, concat_axis=1, tiled=True),
        lax.all_to_all(filter_shared, "dap", split_axis=0, concat_axis=1, tiled=True),
    )
    pair_hat, pair_inv, pair_scaled = standardise_features(
        couple_embedding.astype(jnp.float32), couple_scaling_factor
    )
    pair_ln = pair_scaled.astype(jnp.bfloat16)
    bias_rows = jnp.einsum(
        "ijc,ch->ihj", pair_ln, couple_to_headterm_matrix, preferred_element_type=jnp.float32
    ).astype(jnp.bfloat16)
    couple_headwise_terms = lax.all_gather(bias_rows, "dap", axis=0, tiled=True)

    def onward_loop_step(carry, loop_elements):
        alignment_increment, kept_intermediates = onward_one_line(
            loop_elements[0],
            loop_elements[1],
            couple_headwise_terms,
            alignment_scaling_factor,
            request_matrix,
            lookup_matrix,
            content_matrix,
            switch_matrix,
            final_projection_matrix,
        )
        return (carry, (alignment_increment, kept_intermediates))

    unused_value, (row_updates, all_saved_residuals) = lax.scan(
        onward_loop_step, None, (alignment_line_embedding, alignment_line_flags)
    )
    update_out = lax.all_to_all(row_updates, "dap", split_axis=1, concat_axis=0, tiled=True)
    seq_grad = lax.all_to_all(increment_adjoint, "dap", split_axis=0, concat_axis=1, tiled=True)
    amino_positions = alignment_line_embedding.shape[1]
    span_length = HEAD_NUMBER * HEAD_DIMENSION
    blank_matrix = (
        jnp.zeros((ALIGN_FEATURES, span_length), jnp.float32),
        jnp.zeros((ALIGN_FEATURES, span_length), jnp.float32),
        jnp.zeros((ALIGN_FEATURES, span_length), jnp.float32),
        jnp.zeros((ALIGN_FEATURES, span_length), jnp.float32),
        jnp.zeros((span_length, ALIGN_FEATURES), jnp.float32),
        jnp.zeros((ALIGN_FEATURES,), jnp.float32),
    )

    def backward_step(carry, loop_elements):
        bias_sum, subtotal_list = carry
        line_adjoint, affinity_adjoint, matrix_adjoints = reverse_one_line(
            loop_elements[0],
            loop_elements[1],
            alignment_scaling_factor,
            request_matrix,
            lookup_matrix,
            content_matrix,
            switch_matrix,
            final_projection_matrix,
        )
        subtotal_list = tuple((a + b for a, b in zip(subtotal_list, matrix_adjoints)))
        return ((bias_sum + affinity_adjoint, subtotal_list), line_adjoint)

    beginning_shift = (
        jnp.zeros((amino_positions, HEAD_NUMBER, amino_positions), jnp.float32),
        blank_matrix,
    )
    (bias_term, subtotal_list), line_adjoint_list = lax.scan(
        backward_step, beginning_shift, (seq_grad, all_saved_residuals)
    )
    additive_term_adjoint = lax.psum_scatter(bias_term, "dap", scatter_dimension=0, tiled=True)
    d_pln = jnp.einsum(
        "ihj,ch->ijc",
        additive_term_adjoint,
        couple_to_headterm_matrix.astype(jnp.float32),
        precision=lax.Precision.HIGHEST,
    )
    w_bias_part = jnp.einsum(
        "ijc,ihj->ch",
        pair_ln.astype(jnp.float32),
        additive_term_adjoint,
        precision=lax.Precision.HIGHEST,
    )
    pair_gain_part = jnp.sum(d_pln * pair_hat, axis=(0, 1))
    couple_adjoint = standardise_features_adjoint(
        d_pln, pair_hat, pair_inv, couple_scaling_factor
    ).astype(jnp.bfloat16)
    totals = lax.psum(
        (
            subtotal_list[0],
            subtotal_list[1],
            subtotal_list[2],
            subtotal_list[3],
            subtotal_list[4],
            w_bias_part,
            subtotal_list[5],
            pair_gain_part,
        ),
        "dap",
    )
    alignment_adjoint = lax.all_to_all(
        line_adjoint_list, "dap", split_axis=1, concat_axis=0, tiled=True
    )
    return (
        update_out,
        alignment_adjoint,
        couple_adjoint,
        totals[0],
        totals[1],
        totals[2],
        totals[3],
        totals[4],
        totals[5],
        totals[6],
        totals[7],
    )


def solution(mesh):
    in_specs = (
        P("dp", "dap", None),
        P("dp", "dap"),
        P(("dp", "dap"), None, None),
        P(),
        P(),
        P(),
        P(),
        P(),
        P(),
        P(),
        P(),
        P("dp", "dap", None),
    )
    out_specs = (
        P("dp", "dap", None),
        P("dp", "dap", None),
        P(("dp", "dap"), None, None),
        P("dp", None),
        P("dp", None),
        P("dp", None),
        P("dp", None),
        P("dp", None),
        P("dp", None),
        P("dp"),
        P("dp"),
    )
    return jax.shard_map(
        on_device, mesh=mesh, in_specs=in_specs, out_specs=out_specs, check_vma=False
    )
```

```python
import jax
import jax.numpy as jnp
from jax import lax
from jax.experimental import pallas as pl
from jax.experimental.pallas import tpu as pltpu
from jax.sharding import PartitionSpec as P

ALIGN_FEATURES = 256
HEAD_NUMBER = 8
HEAD_DIMENSION = 32


EPS = 1e-05


def standardise_features(value, gain):
    mean = jnp.mean(value, axis=-1, keepdims=True)
    centered = value - mean
    variance = jnp.mean(centered * centered, axis=-1, keepdims=True)
    reciprocal_spread = lax.rsqrt(variance + EPS)
    standardised_lines = centered * reciprocal_spread
    return (standardised_lines, reciprocal_spread, standardised_lines * gain)


def standardise_features_adjoint(upstream_gradient, standardised_lines, reciprocal_spread, gain):
    rescaled_request = upstream_gradient * gain
    return reciprocal_spread * (
        rescaled_request
        - jnp.mean(rescaled_request, axis=-1, keepdims=True)
        - standardised_lines
        * jnp.mean(rescaled_request * standardised_lines, axis=-1, keepdims=True)
    )


def tensor_product(left, right):
    return lax.dot_general(
        left, right, (((0,), (0,)), ((), ())), preferred_element_type=jnp.float32
    )


def onward_one_line(
    alignment_line_content,
    line_filter_flags,
    couple_headwise_terms,
    alignment_scaling_factor,
    request_matrix,
    lookup_matrix,
    content_matrix,
    switch_matrix,
    final_projection_matrix,
):
    element_number = alignment_line_content.shape[0]
    standardised_lines, reciprocal_spread, rescaled_request = standardise_features(
        alignment_line_content.astype(jnp.float32), alignment_scaling_factor
    )
    input_arrays = rescaled_request.astype(jnp.bfloat16)
    query = (
        jnp.dot(input_arrays, request_matrix, preferred_element_type=jnp.float32)
        * HEAD_DIMENSION ** (-0.5)
    ).astype(jnp.bfloat16)
    keys = jnp.dot(input_arrays, lookup_matrix, preferred_element_type=jnp.float32).astype(
        jnp.bfloat16
    )
    values = jnp.dot(input_arrays, content_matrix, preferred_element_type=jnp.float32).astype(
        jnp.bfloat16
    )
    gate_sigmoid = jax.nn.sigmoid(
        jnp.dot(input_arrays, switch_matrix, preferred_element_type=jnp.float32)
    )
    query = query.reshape(element_number, HEAD_NUMBER, HEAD_DIMENSION)
    keys = keys.reshape(element_number, HEAD_NUMBER, HEAD_DIMENSION)
    values = values.reshape(element_number, HEAD_NUMBER, HEAD_DIMENSION)
    scores = jnp.einsum("ihd,jhd->ihj", query, keys, preferred_element_type=jnp.float32)
    scores = (
        scores
        + couple_headwise_terms.astype(jnp.float32)
        + (1000000000.0 * (line_filter_flags.astype(jnp.float32) - 1.0))[None, None, :]
    )
    probs = jax.nn.softmax(scores, axis=-1)
    probs_low = probs.astype(jnp.bfloat16)
    attention_probs = jnp.einsum(
        "ihj,jhd->ihd", probs_low, values, preferred_element_type=jnp.float32
    ).reshape(element_number, HEAD_NUMBER * HEAD_DIMENSION)
    weighted_values = (gate_sigmoid * attention_probs).astype(jnp.bfloat16)
    alignment_increment = jnp.dot(
        weighted_values, final_projection_matrix, preferred_element_type=jnp.float32
    ).astype(jnp.bfloat16)
    kept_intermediates = (
        standardised_lines,
        reciprocal_spread,
        input_arrays,
        query,
        keys,
        values,
        gate_sigmoid,
        attention_probs,
        weighted_values,
        probs,
    )
    return (alignment_increment, kept_intermediates)


def reverse_one_line(
    line_adjoint_routine,
    kept_intermediates,
    alignment_scaling_factor,
    request_matrix,
    lookup_matrix,
    content_matrix,
    switch_matrix,
    final_projection_matrix,
):
    (
        standardised_lines,
        reciprocal_spread,
        input_arrays,
        query,
        keys,
        values,
        gate_sigmoid,
        attention_probs,
        weighted_values,
        probs,
    ) = kept_intermediates
    element_number = line_adjoint_routine.shape[0]
    probs_low = probs.astype(jnp.bfloat16)
    upstream_gradient = lax.dot_general(
        line_adjoint_routine,
        final_projection_matrix,
        (((1,), (1,)), ((), ())),
        preferred_element_type=jnp.float32,
    )
    d_attn = (upstream_gradient * gate_sigmoid).astype(jnp.bfloat16)
    gate_logit_gradient = (
        upstream_gradient * attention_probs * gate_sigmoid * (1.0 - gate_sigmoid)
    ).astype(jnp.bfloat16)
    d_attn_heads = d_attn.reshape(element_number, HEAD_NUMBER, HEAD_DIMENSION)
    d_probs = jnp.einsum("ihd,jhd->ihj", d_attn_heads, values, preferred_element_type=jnp.float32)
    affinity_adjoint = probs * (d_probs - jnp.sum(probs * d_probs, axis=-1, keepdims=True))
    d_low = affinity_adjoint.astype(jnp.bfloat16)
    query_gradient = (
        (
            jnp.einsum("ihj,jhd->ihd", d_low, keys, preferred_element_type=jnp.float32)
            * HEAD_DIMENSION ** (-0.5)
        )
        .astype(jnp.bfloat16)
        .reshape(element_number, HEAD_NUMBER * HEAD_DIMENSION)
    )
    key_gradient = (
        jnp.einsum("ihj,ihd->jhd", d_low, query, preferred_element_type=jnp.float32)
        .astype(jnp.bfloat16)
        .reshape(element_number, HEAD_NUMBER * HEAD_DIMENSION)
    )
    value_gradient = (
        jnp.einsum("ihj,ihd->jhd", probs_low, d_attn_heads, preferred_element_type=jnp.float32)
        .astype(jnp.bfloat16)
        .reshape(element_number, HEAD_NUMBER * HEAD_DIMENSION)
    )
    backward_result = (((1,), (1,)), ((), ()))
    argument_adjoints = lax.dot_general(
        query_gradient, request_matrix, backward_result, preferred_element_type=jnp.float32
    )
    argument_adjoints = argument_adjoints + lax.dot_general(
        key_gradient, lookup_matrix, backward_result, preferred_element_type=jnp.float32
    )
    argument_adjoints = argument_adjoints + lax.dot_general(
        value_gradient, content_matrix, backward_result, preferred_element_type=jnp.float32
    )
    argument_adjoints = argument_adjoints + lax.dot_general(
        gate_logit_gradient, switch_matrix, backward_result, preferred_element_type=jnp.float32
    )
    line_adjoint = standardise_features_adjoint(
        argument_adjoints, standardised_lines, reciprocal_spread, alignment_scaling_factor
    ).astype(jnp.bfloat16)
    matrix_adjoints = (
        tensor_product(input_arrays, query_gradient),
        tensor_product(input_arrays, key_gradient),
        tensor_product(input_arrays, value_gradient),
        tensor_product(input_arrays, gate_logit_gradient),
        tensor_product(weighted_values, line_adjoint_routine),
        jnp.sum(argument_adjoints * standardised_lines, axis=0),
    )
    return (line_adjoint, affinity_adjoint, matrix_adjoints)


LANES = 128
ROW_TILE = 16


def whole_part_fits(alignment_embedding, couple_embedding):
    sequences, owned, _ = alignment_embedding.shape
    owned_pairs, residues, pair_channels = couple_embedding.shape
    devices = lax.axis_size("dap")
    return (
        owned == 1
        and owned_pairs == 1
        and devices == residues
        and devices % 8 == 0
        and HEAD_NUMBER * residues == LANES
        and pair_channels == LANES
        and sequences == residues
        and sequences % ROW_TILE == 0
    )


def gather_kernel(devices, msa_ref, grad_ref, pair_ref, all_ref, send_sem, recv_sem):
    rows = msa_ref.shape[0]
    me = lax.axis_index("dap")
    planes = devices // 4
    place = lax.rem(me, 4)
    core = lax.rem(place, 2)
    row = place // 2
    sibling = me + 1 - 2 * core
    across = me + 2 - 4 * row
    opposite = me + 3 - 2 * place
    beside = [across, opposite, sibling]
    far = [lax.rem(me + 4 * k, devices) for k in range(1, planes)]
    far_across = [lax.rem(across + 4 * k, devices) for k in range(1, planes)]
    direct = far + far_across[0::2]

    barrier = pltpu.get_barrier_semaphore()
    for peer in direct + beside:
        pl.semaphore_signal(
            barrier, inc=1, device_id={"dap": peer}, device_id_type=pl.DeviceIdType.MESH
        )
    all_ref[me, 0:rows, :] = msa_ref[...]
    all_ref[me, rows : 2 * rows, :] = grad_ref[...]
    all_ref[me, 2 * rows :, :] = pair_ref[...]
    pl.semaphore_wait(barrier, len(direct) + len(beside))

    sent = []

    def send(slot, peer):
        copy = pltpu.make_async_remote_copy(
            src_ref=all_ref.at[slot],
            dst_ref=all_ref.at[slot],
            send_sem=send_sem.at[len(sent)],
            recv_sem=recv_sem.at[slot],
            device_id={"dap": peer},
            device_id_type=pl.DeviceIdType.MESH,
        )
        copy.start()
        sent.append(copy)

    def arrive(slot):
        pltpu.make_async_remote_copy(
            src_ref=all_ref.at[slot],
            dst_ref=all_ref.at[slot],
            send_sem=send_sem.at[0],
            recv_sem=recv_sem.at[slot],
            device_id={"dap": sibling},
            device_id_type=pl.DeviceIdType.MESH,
        ).wait_recv()

    for peer in far[1::2] + [across, opposite] + far[0::2] + far_across[0::2] + [sibling]:
        send(me, peer)
    for slot in far[1::2]:
        arrive(slot)
        for peer in beside:
            send(slot, peer)
    for slot in far[0::2] + far_across[0::2]:
        arrive(slot)
        send(slot, sibling)
    for slot in [across, opposite] + far_across[1::2]:
        arrive(slot)
    for k in range(planes):
        arrive(lax.rem(sibling + 4 * k, devices))
    for k in range(1, planes):
        arrive(lax.rem(opposite + 4 * k, devices))
    for copy in sent:
        copy.wait_send()


def iota(shape, dimension):
    return lax.broadcasted_iota(jnp.int32, shape, dimension)


def one_where(condition):
    return jnp.where(condition, 1.0, 0.0).astype(jnp.bfloat16)


def product(left, right, contract=((1,), (0,))):
    return lax.dot_general(left, right, (contract, ((), ())), preferred_element_type=jnp.float32)


OUTER = ((1,), (1,))
INNER = ((0,), (0,))


def split_product(left, right, contract=((1,), (0,)), split_left=True):
    wide = left if split_left else right
    upper = wide.astype(jnp.bfloat16)
    lower = (wide - upper.astype(jnp.float32)).astype(jnp.bfloat16)
    if split_left:
        return product(upper, right, contract) + product(lower, right, contract)
    return product(left, upper, contract) + product(left, lower, contract)


def over_group(value, width, combine):
    lane = iota(value.shape, 1)
    size = value.shape[1]
    step = 1
    while step < width:
        other = jnp.where(
            (lane // step) % 2 == 0,
            pltpu.roll(value, size - step, 1),
            pltpu.roll(value, step, 1),
        )
        value = combine(value, other)
        step *= 2
    return value


def part_kernel(
    all_ref,
    gain_ref,
    pair_gain_ref,
    request_ref,
    lookup_ref,
    content_ref,
    tail_ref,
    headterm_ref,
    update_ref,
    adjoint_ref,
    pair_adjoint_ref,
    d_query_far,
    d_key_far,
    d_value_far,
    d_gate_far,
    d_out_far,
    d_headterm_ref,
    d_gain_ref,
    d_pair_gain_ref,
    pair_rows_ref,
    d_query_ref,
    d_key_ref,
    d_value_ref,
    d_gate_ref,
    d_out_ref,
    out_sem,
):
    me = lax.axis_index("dap")
    residues = all_ref.shape[0]
    sequences = all_ref.shape[1] // 3
    channels = all_ref.shape[2]
    tokens = residues * sequences
    span = HEAD_NUMBER * HEAD_DIMENSION
    columns = HEAD_NUMBER * residues
    gain = gain_ref[...]
    pair_gain = pair_gain_ref[...]

    pair_lanes = pair_gain.shape[1]
    pair_raw = all_ref[:, 2 * sequences :, 0:pair_lanes].reshape(residues * residues, pair_lanes)
    pair_hat, pair_inv, pair_scaled = standardise_features(
        pair_raw.astype(jnp.float32), pair_gain
    )
    pair_ln = pair_scaled.astype(jnp.bfloat16)
    spread = one_where(
        iota((HEAD_NUMBER, columns), 0) == iota((HEAD_NUMBER, columns), 1) // residues
    )
    headterm_wide = product(headterm_ref[...], spread, INNER).astype(jnp.bfloat16)
    pair_shape = (residues * residues, columns)
    same_key = iota(pair_shape, 0) % residues == iota(pair_shape, 1) % residues
    bias = jnp.sum(
        jnp.where(same_key, product(pair_ln, headterm_wide), 0.0).reshape(
            residues, residues, columns
        ),
        axis=1,
    )
    bias = bias.astype(jnp.bfloat16).astype(jnp.float32)

    flags = all_ref[:, 2 * sequences :, pair_lanes:].astype(jnp.float32)
    flags = flags[:, 0, :].astype(jnp.bfloat16)
    key_shape = (residues, columns)
    flags = product(flags, one_where(iota(key_shape, 0) == iota(key_shape, 1) % residues), INNER)
    fill = 1000000000.0 * (flags[0:sequences] - 1.0)

    square = (tokens, tokens)
    reorder = one_where(
        (iota(square, 0) // residues == iota(square, 1) % sequences)
        & (iota(square, 0) % residues == iota(square, 1) // sequences)
    )
    raw = product(reorder, all_ref[:, 0:sequences, :].reshape(tokens, channels))
    grad = product(
        reorder, all_ref[:, sequences : 2 * sequences, :].reshape(tokens, channels)
    ).astype(jnp.bfloat16)

    hat, inv, scaled = standardise_features(raw, gain)
    x = scaled.astype(jnp.bfloat16)
    query = (product(x, request_ref[...]) * HEAD_DIMENSION ** (-0.5)).astype(jnp.bfloat16)
    keys = product(x, lookup_ref[...]).astype(jnp.bfloat16)
    values = product(x, content_ref[...]).astype(jnp.bfloat16)
    gate = jax.nn.sigmoid(product(x, tail_ref[0:channels, :]))
    upstream = product(grad, tail_ref[channels:, :], OUTER)
    d_attn = (upstream * gate).astype(jnp.bfloat16)

    head_shape = (columns, span)
    own_head = iota(head_shape, 0) // residues == iota(head_shape, 1) // HEAD_DIMENSION
    own_head_one = one_where(own_head)

    def rows_of(value, s):
        return value[s * residues : (s + 1) * residues]

    def by_head(value):
        return jnp.concatenate([value] * HEAD_NUMBER, axis=0) * own_head_one

    def fold_heads(value):
        return jnp.sum(
            jnp.where(own_head, value, 0.0).reshape(HEAD_NUMBER, residues, span), axis=0
        )

    every = range(sequences)
    wide_keys = [by_head(rows_of(keys, s)) for s in every]
    wide_values = [by_head(rows_of(values, s)) for s in every]
    scores = jnp.concatenate(
        [
            product(rows_of(query, s), wide_keys[s], OUTER) + bias + fill[s : s + 1]
            for s in every
        ],
        axis=0,
    )
    scores = jnp.exp(scores - over_group(scores, residues, jnp.maximum))
    probs = scores / over_group(scores, residues, jnp.add)
    probs_low = probs.astype(jnp.bfloat16)
    d_probs = jnp.concatenate(
        [product(rows_of(d_attn, s), wide_values[s], OUTER) for s in every], axis=0
    )
    d_scores = probs * (d_probs - over_group(probs * d_probs, residues, jnp.add))
    d_low = d_scores.astype(jnp.bfloat16)
    attended = jnp.concatenate(
        [product(rows_of(probs_low, s), wide_values[s]) for s in every], axis=0
    )
    weighted = (gate * attended).astype(jnp.bfloat16)
    d_glog = (upstream * attended * gate * (1.0 - gate)).astype(jnp.bfloat16)
    d_query = jnp.concatenate(
        [product(rows_of(d_low, s), wide_keys[s]) for s in every], axis=0
    )
    d_query = (d_query * HEAD_DIMENSION ** (-0.5)).astype(jnp.bfloat16)
    d_keys = jnp.concatenate(
        [fold_heads(product(rows_of(d_low, s), rows_of(query, s), INNER)) for s in every], axis=0
    ).astype(jnp.bfloat16)
    d_values = jnp.concatenate(
        [fold_heads(product(rows_of(probs_low, s), rows_of(d_attn, s), INNER)) for s in every],
        axis=0,
    ).astype(jnp.bfloat16)

    leaving = []
    for near, far, left, right in (
        (d_out_ref, d_out_far, weighted, grad),
        (d_gate_ref, d_gate_far, x, d_glog),
        (d_query_ref, d_query_far, x, d_query),
        (d_key_ref, d_key_far, x, d_keys),
        (d_value_ref, d_value_far, x, d_values),
    ):
        near[...] = product(left, right, INNER)
        copy = pltpu.make_async_copy(near, far, out_sem.at[len(leaving)])
        copy.start()
        leaving.append(copy)

    pick_shape = (sequences, tokens)
    pick = one_where(iota(pick_shape, 1) == iota(pick_shape, 0) * residues + me)
    update_ref[...] = product(
        product(pick, weighted).astype(jnp.bfloat16), tail_ref[channels:, :]
    ).astype(jnp.bfloat16)

    d_x = product(d_query, request_ref[...], OUTER)
    d_x = d_x + product(d_keys, lookup_ref[...], OUTER)
    d_x = d_x + product(d_values, content_ref[...], OUTER)
    d_x = d_x + product(d_glog, tail_ref[0:channels, :], OUTER)
    d_gain_ref[...] = jnp.sum(d_x * hat, axis=0, keepdims=True)
    d_msa = standardise_features_adjoint(d_x, hat, inv, gain).astype(jnp.bfloat16)
    adjoint_ref[...] = product(pick, d_msa).astype(jnp.bfloat16)

    d_bias = jnp.sum(d_scores.reshape(sequences, residues, columns), axis=0)
    d_bias = jnp.where(
        same_key,
        jnp.broadcast_to(d_bias[:, None, :], (residues, residues, columns)).reshape(pair_shape),
        0.0,
    )
    d_pln = split_product(d_bias, headterm_wide, OUTER)
    d_headterm = split_product(pair_ln, d_bias, INNER, split_left=False)
    d_headterm_ref[...] = jnp.sum(
        d_headterm.T.reshape(HEAD_NUMBER, residues, pair_lanes), axis=1
    )
    d_pair_gain_ref[...] = jnp.sum(d_pln * pair_hat, axis=0, keepdims=True)
    pair_rows_ref[...] = (
        standardise_features_adjoint(d_pln, pair_hat, pair_inv, pair_gain)
        .astype(jnp.bfloat16)
        .reshape(residues, residues, pair_lanes)
    )
    pair_adjoint_ref[...] = pair_rows_ref[me]
    for copy in leaving:
        copy.wait()


def on_device_whole_part(
    alignment_embedding,
    alignment_existing_flags,
    couple_embedding,
    alignment_scaling_factor,
    couple_scaling_factor,
    request_matrix,
    lookup_matrix,
    content_matrix,
    switch_matrix,
    final_projection_matrix,
    couple_to_headterm_matrix,
    increment_adjoint,
):
    sequences, _, channels = alignment_embedding.shape
    _, residues, pair_channels = couple_embedding.shape
    devices = lax.axis_size("dap")
    vmem = pl.BlockSpec(memory_space=pltpu.VMEM)
    flags = jnp.pad(
        alignment_existing_flags.T.astype(jnp.bfloat16),
        ((0, 0), (0, channels - pair_channels - sequences)),
    )
    pair_block = jnp.concatenate(
        [
            couple_embedding.reshape(residues, pair_channels),
            jnp.broadcast_to(flags, (residues, channels - pair_channels)),
        ],
        axis=1,
    )
    block_shape = (3 * sequences, channels)
    gathered = pl.pallas_call(
        lambda *refs: gather_kernel(devices, *refs),
        out_shape=jax.ShapeDtypeStruct((devices, *block_shape), jnp.bfloat16),
        in_specs=[vmem] * 3,
        out_specs=vmem,
        scratch_shapes=[
            pltpu.SemaphoreType.DMA((devices - 1,)),
            pltpu.SemaphoreType.DMA((devices,)),
        ],
        compiler_params=pltpu.CompilerParams(
            collective_id=0, has_side_effects=True, vmem_limit_bytes=8 * 1024 * 1024
        ),
        cost_estimate=pl.CostEstimate(
            flops=0, bytes_accessed=100 * devices * 3 * sequences * channels * 2, transcendentals=0
        ),
        name="gather_part",
    )(
        alignment_embedding.reshape(sequences, channels),
        increment_adjoint.reshape(sequences, channels),
        pair_block,
    )
    span = HEAD_NUMBER * HEAD_DIMENSION
    weight = jax.ShapeDtypeStruct((channels, span), jnp.float32)
    outs = pl.pallas_call(
        part_kernel,
        out_shape=(
            jax.ShapeDtypeStruct((sequences, channels), jnp.bfloat16),
            jax.ShapeDtypeStruct((sequences, channels), jnp.bfloat16),
            jax.ShapeDtypeStruct((residues, pair_channels), jnp.bfloat16),
            weight,
            weight,
            weight,
            weight,
            jax.ShapeDtypeStruct((span, channels), jnp.float32),
            jax.ShapeDtypeStruct((HEAD_NUMBER, pair_channels), jnp.float32),
            jax.ShapeDtypeStruct((1, channels), jnp.float32),
            jax.ShapeDtypeStruct((1, pair_channels), jnp.float32),
        ),
        in_specs=[vmem] * 8,
        out_specs=(vmem,) * 3 + (pl.BlockSpec(memory_space=pl.ANY),) * 5 + (vmem,) * 3,
        scratch_shapes=[
            pltpu.VMEM((residues, residues, pair_channels), jnp.bfloat16),
            *[pltpu.VMEM((channels, span), jnp.float32)] * 4,
            pltpu.VMEM((span, channels), jnp.float32),
            pltpu.SemaphoreType.DMA((5,)),
        ],
        compiler_params=pltpu.CompilerParams(vmem_limit_bytes=24 * 1024 * 1024),
        name="whole_part",
    )(
        gathered,
        alignment_scaling_factor.reshape(1, channels),
        couple_scaling_factor.reshape(1, pair_channels),
        request_matrix,
        lookup_matrix,
        content_matrix,
        jnp.concatenate([switch_matrix, final_projection_matrix]),
        couple_to_headterm_matrix.T,
    )
    return (
        outs[0].reshape(alignment_embedding.shape),
        outs[1].reshape(alignment_embedding.shape),
        outs[2].reshape(couple_embedding.shape),
        *outs[3:8],
        outs[8].T,
        outs[9].reshape(channels),
        outs[10].reshape(pair_channels),
    )


def on_device(
    alignment_embedding,
    alignment_existing_flags,
    couple_embedding,
    alignment_scaling_factor,
    couple_scaling_factor,
    request_matrix,
    lookup_matrix,
    content_matrix,
    switch_matrix,
    final_projection_matrix,
    couple_to_headterm_matrix,
    increment_adjoint,
):
    if whole_part_fits(alignment_embedding, couple_embedding):
        return on_device_whole_part(
            alignment_embedding,
            alignment_existing_flags,
            couple_embedding,
            alignment_scaling_factor,
            couple_scaling_factor,
            request_matrix,
            lookup_matrix,
            content_matrix,
            switch_matrix,
            final_projection_matrix,
            couple_to_headterm_matrix,
            increment_adjoint,
        )
    filter_shared = alignment_existing_flags.astype(jnp.bfloat16)
    alignment_line_embedding, alignment_line_flags = (
        lax.all_to_all(alignment_embedding, "dap", split_axis=0, concat_axis=1, tiled=True),
        lax.all_to_all(filter_shared, "dap", split_axis=0, concat_axis=1, tiled=True),
    )
    pair_hat, pair_inv, pair_scaled = standardise_features(
        couple_embedding.astype(jnp.float32), couple_scaling_factor
    )
    pair_ln = pair_scaled.astype(jnp.bfloat16)
    bias_rows = jnp.einsum(
        "ijc,ch->ihj", pair_ln, couple_to_headterm_matrix, preferred_element_type=jnp.float32
    ).astype(jnp.bfloat16)
    couple_headwise_terms = lax.all_gather(bias_rows, "dap", axis=0, tiled=True)

    def onward_loop_step(carry, loop_elements):
        alignment_increment, kept_intermediates = onward_one_line(
            loop_elements[0],
            loop_elements[1],
            couple_headwise_terms,
            alignment_scaling_factor,
            request_matrix,
            lookup_matrix,
            content_matrix,
            switch_matrix,
            final_projection_matrix,
        )
        return (carry, (alignment_increment, kept_intermediates))

    unused_value, (row_updates, all_saved_residuals) = lax.scan(
        onward_loop_step, None, (alignment_line_embedding, alignment_line_flags)
    )
    update_out = lax.all_to_all(row_updates, "dap", split_axis=1, concat_axis=0, tiled=True)
    seq_grad = lax.all_to_all(increment_adjoint, "dap", split_axis=0, concat_axis=1, tiled=True)
    amino_positions = alignment_line_embedding.shape[1]
    span_length = HEAD_NUMBER * HEAD_DIMENSION
    blank_matrix = (
        jnp.zeros((ALIGN_FEATURES, span_length), jnp.float32),
        jnp.zeros((ALIGN_FEATURES, span_length), jnp.float32),
        jnp.zeros((ALIGN_FEATURES, span_length), jnp.float32),
        jnp.zeros((ALIGN_FEATURES, span_length), jnp.float32),
        jnp.zeros((span_length, ALIGN_FEATURES), jnp.float32),
        jnp.zeros((ALIGN_FEATURES,), jnp.float32),
    )

    def backward_step(carry, loop_elements):
        bias_sum, subtotal_list = carry
        line_adjoint, affinity_adjoint, matrix_adjoints = reverse_one_line(
            loop_elements[0],
            loop_elements[1],
            alignment_scaling_factor,
            request_matrix,
            lookup_matrix,
            content_matrix,
            switch_matrix,
            final_projection_matrix,
        )
        subtotal_list = tuple((a + b for a, b in zip(subtotal_list, matrix_adjoints)))
        return ((bias_sum + affinity_adjoint, subtotal_list), line_adjoint)

    beginning_shift = (
        jnp.zeros((amino_positions, HEAD_NUMBER, amino_positions), jnp.float32),
        blank_matrix,
    )
    (bias_term, subtotal_list), line_adjoint_list = lax.scan(
        backward_step, beginning_shift, (seq_grad, all_saved_residuals)
    )
    additive_term_adjoint = lax.psum_scatter(bias_term, "dap", scatter_dimension=0, tiled=True)
    d_pln = jnp.einsum(
        "ihj,ch->ijc",
        additive_term_adjoint,
        couple_to_headterm_matrix.astype(jnp.float32),
        precision=lax.Precision.HIGHEST,
    )
    w_bias_part = jnp.einsum(
        "ijc,ihj->ch",
        pair_ln.astype(jnp.float32),
        additive_term_adjoint,
        precision=lax.Precision.HIGHEST,
    )
    pair_gain_part = jnp.sum(d_pln * pair_hat, axis=(0, 1))
    couple_adjoint = standardise_features_adjoint(
        d_pln, pair_hat, pair_inv, couple_scaling_factor
    ).astype(jnp.bfloat16)
    totals = lax.psum(
        (
            subtotal_list[0],
            subtotal_list[1],
            subtotal_list[2],
            subtotal_list[3],
            subtotal_list[4],
            w_bias_part,
            subtotal_list[5],
            pair_gain_part,
        ),
        "dap",
    )
    alignment_adjoint = lax.all_to_all(
        line_adjoint_list, "dap", split_axis=1, concat_axis=0, tiled=True
    )
    return (
        update_out,
        alignment_adjoint,
        couple_adjoint,
        totals[0],
        totals[1],
        totals[2],
        totals[3],
        totals[4],
        totals[5],
        totals[6],
        totals[7],
    )


def solution(mesh):
    in_specs = (
        P("dp", "dap", None),
        P("dp", "dap"),
        P(("dp", "dap"), None, None),
        P(),
        P(),
        P(),
        P(),
        P(),
        P(),
        P(),
        P(),
        P("dp", "dap", None),
    )
    out_specs = (
        P("dp", "dap", None),
        P("dp", "dap", None),
        P(("dp", "dap"), None, None),
        P("dp", None),
        P("dp", None),
        P("dp", None),
        P("dp", None),
        P("dp", None),
        P("dp", None),
        P("dp"),
        P("dp"),
    )
    return jax.shard_map(
        on_device, mesh=mesh, in_specs=in_specs, out_specs=out_specs, check_vma=False
    )
```

```python
import jax
import jax.numpy as jnp
from jax import lax
from jax.experimental import pallas as pl
from jax.experimental.pallas import tpu as pltpu
from jax.sharding import PartitionSpec as P

ALIGN_FEATURES = 256
HEAD_NUMBER = 8
HEAD_DIMENSION = 32


EPS = 1e-05


def standardise_features(value, gain):
    mean = jnp.mean(value, axis=-1, keepdims=True)
    centered = value - mean
    variance = jnp.mean(centered * centered, axis=-1, keepdims=True)
    reciprocal_spread = lax.rsqrt(variance + EPS)
    standardised_lines = centered * reciprocal_spread
    return (standardised_lines, reciprocal_spread, standardised_lines * gain)


def standardise_features_adjoint(upstream_gradient, standardised_lines, reciprocal_spread, gain):
    rescaled_request = upstream_gradient * gain
    return reciprocal_spread * (
        rescaled_request
        - jnp.mean(rescaled_request, axis=-1, keepdims=True)
        - standardised_lines
        * jnp.mean(rescaled_request * standardised_lines, axis=-1, keepdims=True)
    )


def tensor_product(left, right):
    return lax.dot_general(
        left, right, (((0,), (0,)), ((), ())), preferred_element_type=jnp.float32
    )


def onward_one_line(
    alignment_line_content,
    line_filter_flags,
    couple_headwise_terms,
    alignment_scaling_factor,
    request_matrix,
    lookup_matrix,
    content_matrix,
    switch_matrix,
    final_projection_matrix,
):
    element_number = alignment_line_content.shape[0]
    standardised_lines, reciprocal_spread, rescaled_request = standardise_features(
        alignment_line_content.astype(jnp.float32), alignment_scaling_factor
    )
    input_arrays = rescaled_request.astype(jnp.bfloat16)
    query = (
        jnp.dot(input_arrays, request_matrix, preferred_element_type=jnp.float32)
        * HEAD_DIMENSION ** (-0.5)
    ).astype(jnp.bfloat16)
    keys = jnp.dot(input_arrays, lookup_matrix, preferred_element_type=jnp.float32).astype(
        jnp.bfloat16
    )
    values = jnp.dot(input_arrays, content_matrix, preferred_element_type=jnp.float32).astype(
        jnp.bfloat16
    )
    gate_sigmoid = jax.nn.sigmoid(
        jnp.dot(input_arrays, switch_matrix, preferred_element_type=jnp.float32)
    )
    query = query.reshape(element_number, HEAD_NUMBER, HEAD_DIMENSION)
    keys = keys.reshape(element_number, HEAD_NUMBER, HEAD_DIMENSION)
    values = values.reshape(element_number, HEAD_NUMBER, HEAD_DIMENSION)
    scores = jnp.einsum("ihd,jhd->ihj", query, keys, preferred_element_type=jnp.float32)
    scores = (
        scores
        + couple_headwise_terms.astype(jnp.float32)
        + (1000000000.0 * (line_filter_flags.astype(jnp.float32) - 1.0))[None, None, :]
    )
    probs = jax.nn.softmax(scores, axis=-1)
    probs_low = probs.astype(jnp.bfloat16)
    attention_probs = jnp.einsum(
        "ihj,jhd->ihd", probs_low, values, preferred_element_type=jnp.float32
    ).reshape(element_number, HEAD_NUMBER * HEAD_DIMENSION)
    weighted_values = (gate_sigmoid * attention_probs).astype(jnp.bfloat16)
    alignment_increment = jnp.dot(
        weighted_values, final_projection_matrix, preferred_element_type=jnp.float32
    ).astype(jnp.bfloat16)
    kept_intermediates = (
        standardised_lines,
        reciprocal_spread,
        input_arrays,
        query,
        keys,
        values,
        gate_sigmoid,
        attention_probs,
        weighted_values,
        probs,
    )
    return (alignment_increment, kept_intermediates)


def reverse_one_line(
    line_adjoint_routine,
    kept_intermediates,
    alignment_scaling_factor,
    request_matrix,
    lookup_matrix,
    content_matrix,
    switch_matrix,
    final_projection_matrix,
):
    (
        standardised_lines,
        reciprocal_spread,
        input_arrays,
        query,
        keys,
        values,
        gate_sigmoid,
        attention_probs,
        weighted_values,
        probs,
    ) = kept_intermediates
    element_number = line_adjoint_routine.shape[0]
    probs_low = probs.astype(jnp.bfloat16)
    upstream_gradient = lax.dot_general(
        line_adjoint_routine,
        final_projection_matrix,
        (((1,), (1,)), ((), ())),
        preferred_element_type=jnp.float32,
    )
    d_attn = (upstream_gradient * gate_sigmoid).astype(jnp.bfloat16)
    gate_logit_gradient = (
        upstream_gradient * attention_probs * gate_sigmoid * (1.0 - gate_sigmoid)
    ).astype(jnp.bfloat16)
    d_attn_heads = d_attn.reshape(element_number, HEAD_NUMBER, HEAD_DIMENSION)
    d_probs = jnp.einsum("ihd,jhd->ihj", d_attn_heads, values, preferred_element_type=jnp.float32)
    affinity_adjoint = probs * (d_probs - jnp.sum(probs * d_probs, axis=-1, keepdims=True))
    d_low = affinity_adjoint.astype(jnp.bfloat16)
    query_gradient = (
        (
            jnp.einsum("ihj,jhd->ihd", d_low, keys, preferred_element_type=jnp.float32)
            * HEAD_DIMENSION ** (-0.5)
        )
        .astype(jnp.bfloat16)
        .reshape(element_number, HEAD_NUMBER * HEAD_DIMENSION)
    )
    key_gradient = (
        jnp.einsum("ihj,ihd->jhd", d_low, query, preferred_element_type=jnp.float32)
        .astype(jnp.bfloat16)
        .reshape(element_number, HEAD_NUMBER * HEAD_DIMENSION)
    )
    value_gradient = (
        jnp.einsum("ihj,ihd->jhd", probs_low, d_attn_heads, preferred_element_type=jnp.float32)
        .astype(jnp.bfloat16)
        .reshape(element_number, HEAD_NUMBER * HEAD_DIMENSION)
    )
    backward_result = (((1,), (1,)), ((), ()))
    argument_adjoints = lax.dot_general(
        query_gradient, request_matrix, backward_result, preferred_element_type=jnp.float32
    )
    argument_adjoints = argument_adjoints + lax.dot_general(
        key_gradient, lookup_matrix, backward_result, preferred_element_type=jnp.float32
    )
    argument_adjoints = argument_adjoints + lax.dot_general(
        value_gradient, content_matrix, backward_result, preferred_element_type=jnp.float32
    )
    argument_adjoints = argument_adjoints + lax.dot_general(
        gate_logit_gradient, switch_matrix, backward_result, preferred_element_type=jnp.float32
    )
    line_adjoint = standardise_features_adjoint(
        argument_adjoints, standardised_lines, reciprocal_spread, alignment_scaling_factor
    ).astype(jnp.bfloat16)
    matrix_adjoints = (
        tensor_product(input_arrays, query_gradient),
        tensor_product(input_arrays, key_gradient),
        tensor_product(input_arrays, value_gradient),
        tensor_product(input_arrays, gate_logit_gradient),
        tensor_product(weighted_values, line_adjoint_routine),
        jnp.sum(argument_adjoints * standardised_lines, axis=0),
    )
    return (line_adjoint, affinity_adjoint, matrix_adjoints)


LANES = 128
ROW_TILE = 16


def whole_part_fits(alignment_embedding, couple_embedding):
    sequences, owned, _ = alignment_embedding.shape
    owned_pairs, residues, pair_channels = couple_embedding.shape
    devices = lax.axis_size("dap")
    return (
        owned == 1
        and owned_pairs == 1
        and devices == residues
        and devices % 8 == 0
        and HEAD_NUMBER * residues == LANES
        and pair_channels == LANES
        and sequences == residues
        and sequences % ROW_TILE == 0
    )


def gather_kernel(devices, msa_ref, grad_ref, pair_ref, all_ref, send_sem, recv_sem):
    rows = msa_ref.shape[0]
    me = lax.axis_index("dap")
    planes = devices // 4
    place = lax.rem(me, 4)
    core = lax.rem(place, 2)
    row = place // 2
    sibling = me + 1 - 2 * core
    across = me + 2 - 4 * row
    opposite = me + 3 - 2 * place
    beside = [across, opposite, sibling]
    far = [lax.rem(me + 4 * k, devices) for k in range(1, planes)]
    far_across = [lax.rem(across + 4 * k, devices) for k in range(1, planes)]
    direct = far + far_across[0::2]

    barrier = pltpu.get_barrier_semaphore()
    for peer in direct + beside:
        pl.semaphore_signal(
            barrier, inc=1, device_id={"dap": peer}, device_id_type=pl.DeviceIdType.MESH
        )
    all_ref[me, 0:rows, :] = msa_ref[...]
    all_ref[me, rows : 2 * rows, :] = grad_ref[...]
    all_ref[me, 2 * rows :, :] = pair_ref[...]
    pl.semaphore_wait(barrier, len(direct) + len(beside))

    sent = []

    def send(slot, peer):
        copy = pltpu.make_async_remote_copy(
            src_ref=all_ref.at[slot],
            dst_ref=all_ref.at[slot],
            send_sem=send_sem.at[len(sent)],
            recv_sem=recv_sem.at[slot],
            device_id={"dap": peer},
            device_id_type=pl.DeviceIdType.MESH,
        )
        copy.start()
        sent.append(copy)

    def arrive(slot):
        pltpu.make_async_remote_copy(
            src_ref=all_ref.at[slot],
            dst_ref=all_ref.at[slot],
            send_sem=send_sem.at[0],
            recv_sem=recv_sem.at[slot],
            device_id={"dap": sibling},
            device_id_type=pl.DeviceIdType.MESH,
        ).wait_recv()

    for peer in far[1::2] + [across] + far[0::2] + far_across[0::2] + [sibling]:
        send(me, peer)
    arrive(across)
    send(across, sibling)
    for slot in far[1::2]:
        arrive(slot)
        for peer in beside:
            send(slot, peer)
    for slot in far[0::2] + far_across[0::2]:
        arrive(slot)
        send(slot, sibling)
    for slot in far_across[1::2]:
        arrive(slot)
    for k in range(planes):
        arrive(lax.rem(sibling + 4 * k, devices))
        arrive(lax.rem(opposite + 4 * k, devices))
    for copy in sent:
        copy.wait_send()


def iota(shape, dimension):
    return lax.broadcasted_iota(jnp.int32, shape, dimension)


def one_where(condition):
    return jnp.where(condition, 1.0, 0.0).astype(jnp.bfloat16)


def product(left, right, contract=((1,), (0,))):
    return lax.dot_general(left, right, (contract, ((), ())), preferred_element_type=jnp.float32)


OUTER = ((1,), (1,))
INNER = ((0,), (0,))


def split_product(left, right, contract=((1,), (0,)), split_left=True):
    wide = left if split_left else right
    upper = wide.astype(jnp.bfloat16)
    lower = (wide - upper.astype(jnp.float32)).astype(jnp.bfloat16)
    if split_left:
        return product(upper, right, contract) + product(lower, right, contract)
    return product(left, upper, contract) + product(left, lower, contract)


def over_group(value, width, combine):
    lane = iota(value.shape, 1)
    size = value.shape[1]
    step = 1
    while step < width:
        other = jnp.where(
            (lane // step) % 2 == 0,
            pltpu.roll(value, size - step, 1),
            pltpu.roll(value, step, 1),
        )
        value = combine(value, other)
        step *= 2
    return value


def part_kernel(
    all_ref,
    gain_ref,
    pair_gain_ref,
    request_ref,
    lookup_ref,
    content_ref,
    tail_ref,
    headterm_ref,
    update_ref,
    adjoint_ref,
    pair_adjoint_ref,
    d_query_ref,
    d_key_ref,
    d_value_ref,
    d_gate_ref,
    d_out_ref,
    d_headterm_ref,
    d_gain_ref,
    d_pair_gain_ref,
    pair_rows_ref,
):
    me = lax.axis_index("dap")
    residues = all_ref.shape[0]
    sequences = all_ref.shape[1] // 3
    channels = all_ref.shape[2]
    tokens = residues * sequences
    span = HEAD_NUMBER * HEAD_DIMENSION
    columns = HEAD_NUMBER * residues
    gain = gain_ref[...]
    pair_gain = pair_gain_ref[...]

    pair_lanes = pair_gain.shape[1]
    pair_raw = all_ref[:, 2 * sequences :, 0:pair_lanes].reshape(residues * residues, pair_lanes)
    pair_hat, pair_inv, pair_scaled = standardise_features(
        pair_raw.astype(jnp.float32), pair_gain
    )
    pair_ln = pair_scaled.astype(jnp.bfloat16)
    spread = one_where(
        iota((HEAD_NUMBER, columns), 0) == iota((HEAD_NUMBER, columns), 1) // residues
    )
    headterm_wide = product(headterm_ref[...], spread, INNER).astype(jnp.bfloat16)
    pair_shape = (residues * residues, columns)
    same_key = iota(pair_shape, 0) % residues == iota(pair_shape, 1) % residues
    bias = jnp.sum(
        jnp.where(same_key, product(pair_ln, headterm_wide), 0.0).reshape(
            residues, residues, columns
        ),
        axis=1,
    )
    bias = bias.astype(jnp.bfloat16).astype(jnp.float32)

    flags = all_ref[:, 2 * sequences :, pair_lanes:].astype(jnp.float32)
    flags = flags[:, 0, :].astype(jnp.bfloat16)
    key_shape = (residues, columns)
    flags = product(flags, one_where(iota(key_shape, 0) == iota(key_shape, 1) % residues), INNER)
    fill = 1000000000.0 * (flags[0:sequences] - 1.0)

    square = (tokens, tokens)
    reorder = one_where(
        (iota(square, 0) // residues == iota(square, 1) % sequences)
        & (iota(square, 0) % residues == iota(square, 1) // sequences)
    )
    raw = product(reorder, all_ref[:, 0:sequences, :].reshape(tokens, channels))
    grad = product(
        reorder, all_ref[:, sequences : 2 * sequences, :].reshape(tokens, channels)
    ).astype(jnp.bfloat16)

    hat, inv, scaled = standardise_features(raw, gain)
    x = scaled.astype(jnp.bfloat16)
    query = (product(x, request_ref[...]) * HEAD_DIMENSION ** (-0.5)).astype(jnp.bfloat16)
    keys = product(x, lookup_ref[...]).astype(jnp.bfloat16)
    values = product(x, content_ref[...]).astype(jnp.bfloat16)
    gate = jax.nn.sigmoid(product(x, tail_ref[0:channels, :]))
    upstream = product(grad, tail_ref[channels:, :], OUTER)
    d_attn = (upstream * gate).astype(jnp.bfloat16)

    head_shape = (columns, span)
    own_head = iota(head_shape, 0) // residues == iota(head_shape, 1) // HEAD_DIMENSION
    own_head_one = one_where(own_head)

    def rows_of(value, s):
        return value[s * residues : (s + 1) * residues]

    def by_head(value):
        return jnp.concatenate([value] * HEAD_NUMBER, axis=0) * own_head_one

    def fold_heads(value):
        return jnp.sum(
            jnp.where(own_head, value, 0.0).reshape(HEAD_NUMBER, residues, span), axis=0
        )

    every = range(sequences)
    wide_keys = [by_head(rows_of(keys, s)) for s in every]
    wide_values = [by_head(rows_of(values, s)) for s in every]
    scores = jnp.concatenate(
        [
            product(rows_of(query, s), wide_keys[s], OUTER) + bias + fill[s : s + 1]
            for s in every
        ],
        axis=0,
    )
    scores = jnp.exp(scores - over_group(scores, residues, jnp.maximum))
    probs = scores / over_group(scores, residues, jnp.add)
    probs_low = probs.astype(jnp.bfloat16)
    d_probs = jnp.concatenate(
        [product(rows_of(d_attn, s), wide_values[s], OUTER) for s in every], axis=0
    )
    d_scores = probs * (d_probs - over_group(probs * d_probs, residues, jnp.add))
    d_low = d_scores.astype(jnp.bfloat16)
    attended = jnp.concatenate(
        [product(rows_of(probs_low, s), wide_values[s]) for s in every], axis=0
    )
    weighted = (gate * attended).astype(jnp.bfloat16)
    d_glog = (upstream * attended * gate * (1.0 - gate)).astype(jnp.bfloat16)
    d_query = jnp.concatenate(
        [product(rows_of(d_low, s), wide_keys[s]) for s in every], axis=0
    )
    d_query = (d_query * HEAD_DIMENSION ** (-0.5)).astype(jnp.bfloat16)
    d_keys = jnp.concatenate(
        [fold_heads(product(rows_of(d_low, s), rows_of(query, s), INNER)) for s in every], axis=0
    ).astype(jnp.bfloat16)
    d_values = jnp.concatenate(
        [fold_heads(product(rows_of(probs_low, s), rows_of(d_attn, s), INNER)) for s in every],
        axis=0,
    ).astype(jnp.bfloat16)

    d_query_ref[...] = product(x, d_query, INNER)
    d_key_ref[...] = product(x, d_keys, INNER)
    d_value_ref[...] = product(x, d_values, INNER)
    d_gate_ref[...] = product(x, d_glog, INNER)
    d_out_ref[...] = product(weighted, grad, INNER)

    pick_shape = (sequences, tokens)
    pick = one_where(iota(pick_shape, 1) == iota(pick_shape, 0) * residues + me)
    update_ref[...] = product(
        product(pick, weighted).astype(jnp.bfloat16), tail_ref[channels:, :]
    ).astype(jnp.bfloat16)

    d_x = product(d_query, request_ref[...], OUTER)
    d_x = d_x + product(d_keys, lookup_ref[...], OUTER)
    d_x = d_x + product(d_values, content_ref[...], OUTER)
    d_x = d_x + product(d_glog, tail_ref[0:channels, :], OUTER)
    d_gain_ref[...] = jnp.sum(d_x * hat, axis=0, keepdims=True)
    d_msa = standardise_features_adjoint(d_x, hat, inv, gain).astype(jnp.bfloat16)
    adjoint_ref[...] = product(pick, d_msa).astype(jnp.bfloat16)

    d_bias = jnp.sum(d_scores.reshape(sequences, residues, columns), axis=0)
    d_bias = jnp.where(
        same_key,
        jnp.broadcast_to(d_bias[:, None, :], (residues, residues, columns)).reshape(pair_shape),
        0.0,
    )
    d_pln = split_product(d_bias, headterm_wide, OUTER)
    d_headterm = split_product(pair_ln, d_bias, INNER, split_left=False)
    d_headterm_ref[...] = jnp.sum(
        d_headterm.T.reshape(HEAD_NUMBER, residues, pair_lanes), axis=1
    )
    d_pair_gain_ref[...] = jnp.sum(d_pln * pair_hat, axis=0, keepdims=True)
    pair_rows_ref[...] = (
        standardise_features_adjoint(d_pln, pair_hat, pair_inv, pair_gain)
        .astype(jnp.bfloat16)
        .reshape(residues, residues, pair_lanes)
    )
    pair_adjoint_ref[...] = pair_rows_ref[me]


def on_device_whole_part(
    alignment_embedding,
    alignment_existing_flags,
    couple_embedding,
    alignment_scaling_factor,
    couple_scaling_factor,
    request_matrix,
    lookup_matrix,
    content_matrix,
    switch_matrix,
    final_projection_matrix,
    couple_to_headterm_matrix,
    increment_adjoint,
):
    sequences, _, channels = alignment_embedding.shape
    _, residues, pair_channels = couple_embedding.shape
    devices = lax.axis_size("dap")
    vmem = pl.BlockSpec(memory_space=pltpu.VMEM)
    flags = jnp.pad(
        alignment_existing_flags.T.astype(jnp.bfloat16),
        ((0, 0), (0, channels - pair_channels - sequences)),
    )
    pair_block = jnp.concatenate(
        [
            couple_embedding.reshape(residues, pair_channels),
            jnp.broadcast_to(flags, (residues, channels - pair_channels)),
        ],
        axis=1,
    )
    block_shape = (3 * sequences, channels)
    gathered = pl.pallas_call(
        lambda *refs: gather_kernel(devices, *refs),
        out_shape=jax.ShapeDtypeStruct((devices, *block_shape), jnp.bfloat16),
        in_specs=[vmem] * 3,
        out_specs=vmem,
        scratch_shapes=[
            pltpu.SemaphoreType.DMA((devices - 1,)),
            pltpu.SemaphoreType.DMA((devices,)),
        ],
        compiler_params=pltpu.CompilerParams(
            collective_id=0, has_side_effects=True, vmem_limit_bytes=8 * 1024 * 1024
        ),
        cost_estimate=pl.CostEstimate(
            flops=0, bytes_accessed=100 * devices * 3 * sequences * channels * 2, transcendentals=0
        ),
        name="gather_part",
    )(
        alignment_embedding.reshape(sequences, channels),
        increment_adjoint.reshape(sequences, channels),
        pair_block,
    )
    span = HEAD_NUMBER * HEAD_DIMENSION
    weight = jax.ShapeDtypeStruct((channels, span), jnp.float32)
    outs = pl.pallas_call(
        part_kernel,
        out_shape=(
            jax.ShapeDtypeStruct((sequences, channels), jnp.bfloat16),
            jax.ShapeDtypeStruct((sequences, channels), jnp.bfloat16),
            jax.ShapeDtypeStruct((residues, pair_channels), jnp.bfloat16),
            weight,
            weight,
            weight,
            weight,
            jax.ShapeDtypeStruct((span, channels), jnp.float32),
            jax.ShapeDtypeStruct((HEAD_NUMBER, pair_channels), jnp.float32),
            jax.ShapeDtypeStruct((1, channels), jnp.float32),
            jax.ShapeDtypeStruct((1, pair_channels), jnp.float32),
        ),
        in_specs=[vmem] * 8,
        out_specs=(vmem,) * 11,
        scratch_shapes=[pltpu.VMEM((residues, residues, pair_channels), jnp.bfloat16)],
        compiler_params=pltpu.CompilerParams(vmem_limit_bytes=24 * 1024 * 1024),
        name="whole_part",
    )(
        gathered,
        alignment_scaling_factor.reshape(1, channels),
        couple_scaling_factor.reshape(1, pair_channels),
        request_matrix,
        lookup_matrix,
        content_matrix,
        jnp.concatenate([switch_matrix, final_projection_matrix]),
        couple_to_headterm_matrix.T,
    )
    return (
        outs[0].reshape(alignment_embedding.shape),
        outs[1].reshape(alignment_embedding.shape),
        outs[2].reshape(couple_embedding.shape),
        *outs[3:8],
        outs[8].T,
        outs[9].reshape(channels),
        outs[10].reshape(pair_channels),
    )


def on_device(
    alignment_embedding,
    alignment_existing_flags,
    couple_embedding,
    alignment_scaling_factor,
    couple_scaling_factor,
    request_matrix,
    lookup_matrix,
    content_matrix,
    switch_matrix,
    final_projection_matrix,
    couple_to_headterm_matrix,
    increment_adjoint,
):
    if whole_part_fits(alignment_embedding, couple_embedding):
        return on_device_whole_part(
            alignment_embedding,
            alignment_existing_flags,
            couple_embedding,
            alignment_scaling_factor,
            couple_scaling_factor,
            request_matrix,
            lookup_matrix,
            content_matrix,
            switch_matrix,
            final_projection_matrix,
            couple_to_headterm_matrix,
            increment_adjoint,
        )
    filter_shared = alignment_existing_flags.astype(jnp.bfloat16)
    alignment_line_embedding, alignment_line_flags = (
        lax.all_to_all(alignment_embedding, "dap", split_axis=0, concat_axis=1, tiled=True),
        lax.all_to_all(filter_shared, "dap", split_axis=0, concat_axis=1, tiled=True),
    )
    pair_hat, pair_inv, pair_scaled = standardise_features(
        couple_embedding.astype(jnp.float32), couple_scaling_factor
    )
    pair_ln = pair_scaled.astype(jnp.bfloat16)
    bias_rows = jnp.einsum(
        "ijc,ch->ihj", pair_ln, couple_to_headterm_matrix, preferred_element_type=jnp.float32
    ).astype(jnp.bfloat16)
    couple_headwise_terms = lax.all_gather(bias_rows, "dap", axis=0, tiled=True)

    def onward_loop_step(carry, loop_elements):
        alignment_increment, kept_intermediates = onward_one_line(
            loop_elements[0],
            loop_elements[1],
            couple_headwise_terms,
            alignment_scaling_factor,
            request_matrix,
            lookup_matrix,
            content_matrix,
            switch_matrix,
            final_projection_matrix,
        )
        return (carry, (alignment_increment, kept_intermediates))

    unused_value, (row_updates, all_saved_residuals) = lax.scan(
        onward_loop_step, None, (alignment_line_embedding, alignment_line_flags)
    )
    update_out = lax.all_to_all(row_updates, "dap", split_axis=1, concat_axis=0, tiled=True)
    seq_grad = lax.all_to_all(increment_adjoint, "dap", split_axis=0, concat_axis=1, tiled=True)
    amino_positions = alignment_line_embedding.shape[1]
    span_length = HEAD_NUMBER * HEAD_DIMENSION
    blank_matrix = (
        jnp.zeros((ALIGN_FEATURES, span_length), jnp.float32),
        jnp.zeros((ALIGN_FEATURES, span_length), jnp.float32),
        jnp.zeros((ALIGN_FEATURES, span_length), jnp.float32),
        jnp.zeros((ALIGN_FEATURES, span_length), jnp.float32),
        jnp.zeros((span_length, ALIGN_FEATURES), jnp.float32),
        jnp.zeros((ALIGN_FEATURES,), jnp.float32),
    )

    def backward_step(carry, loop_elements):
        bias_sum, subtotal_list = carry
        line_adjoint, affinity_adjoint, matrix_adjoints = reverse_one_line(
            loop_elements[0],
            loop_elements[1],
            alignment_scaling_factor,
            request_matrix,
            lookup_matrix,
            content_matrix,
            switch_matrix,
            final_projection_matrix,
        )
        subtotal_list = tuple((a + b for a, b in zip(subtotal_list, matrix_adjoints)))
        return ((bias_sum + affinity_adjoint, subtotal_list), line_adjoint)

    beginning_shift = (
        jnp.zeros((amino_positions, HEAD_NUMBER, amino_positions), jnp.float32),
        blank_matrix,
    )
    (bias_term, subtotal_list), line_adjoint_list = lax.scan(
        backward_step, beginning_shift, (seq_grad, all_saved_residuals)
    )
    additive_term_adjoint = lax.psum_scatter(bias_term, "dap", scatter_dimension=0, tiled=True)
    d_pln = jnp.einsum(
        "ihj,ch->ijc",
        additive_term_adjoint,
        couple_to_headterm_matrix.astype(jnp.float32),
        precision=lax.Precision.HIGHEST,
    )
    w_bias_part = jnp.einsum(
        "ijc,ihj->ch",
        pair_ln.astype(jnp.float32),
        additive_term_adjoint,
        precision=lax.Precision.HIGHEST,
    )
    pair_gain_part = jnp.sum(d_pln * pair_hat, axis=(0, 1))
    couple_adjoint = standardise_features_adjoint(
        d_pln, pair_hat, pair_inv, couple_scaling_factor
    ).astype(jnp.bfloat16)
    totals = lax.psum(
        (
            subtotal_list[0],
            subtotal_list[1],
            subtotal_list[2],
            subtotal_list[3],
            subtotal_list[4],
            w_bias_part,
            subtotal_list[5],
            pair_gain_part,
        ),
        "dap",
    )
    alignment_adjoint = lax.all_to_all(
        line_adjoint_list, "dap", split_axis=1, concat_axis=0, tiled=True
    )
    return (
        update_out,
        alignment_adjoint,
        couple_adjoint,
        totals[0],
        totals[1],
        totals[2],
        totals[3],
        totals[4],
        totals[5],
        totals[6],
        totals[7],
    )


def solution(mesh):
    in_specs = (
        P("dp", "dap", None),
        P("dp", "dap"),
        P(("dp", "dap"), None, None),
        P(),
        P(),
        P(),
        P(),
        P(),
        P(),
        P(),
        P(),
        P("dp", "dap", None),
    )
    out_specs = (
        P("dp", "dap", None),
        P("dp", "dap", None),
        P(("dp", "dap"), None, None),
        P("dp", None),
        P("dp", None),
        P("dp", None),
        P("dp", None),
        P("dp", None),
        P("dp", None),
        P("dp"),
        P("dp"),
    )
    return jax.shard_map(
        on_device, mesh=mesh, in_specs=in_specs, out_specs=out_specs, check_vma=False
    )
```
